32 devices in a mesh: batch: 4 (over y, x), ctx: 8 (over z, core).
Axes of the slice: x: 2, y: 2, z: 4, core: 2. Of those that a mesh axis runs over, the one named last changes fastest.
Arguments:
- tokens: bfloat16 [16, 1024, 640], P('batch', 'ctx'), may hold values from -6 to 6
- w_qkv: bfloat16 [640, 1536], P('ctx', 'batch'), may hold values from -0.25 to 0.25
- w_out: bfloat16 [1024, 640], P('batch', 'ctx'), may hold values from -0.1875 to 0.1875
- w_gate_up: bfloat16 [640, 4096], P('ctx', 'batch'), may hold values from -0.25 to 0.25
- w_down: bfloat16 [2048, 640], P('batch', 'ctx'), may hold values from -0.125 to 0.125
- norm_gains: bfloat16 [3072], P(('batch', 'ctx')), may hold values from -0.5 to 0.5
- block_order: int32 [16], replicated, may hold values from 0 to 15, as said below
- cotangent: bfloat16 [16, 1024, 640], P('batch', 'ctx'), may hold values from -6 to 6
Outputs:
- output: bfloat16 [16, 1024, 640], P('batch', 'ctx')
- grad_tokens: float32 [16, 1024, 640], P('batch', 'ctx')
- grad_w_qkv: float32 [640, 1536], P('ctx', 'batch')
- grad_w_out: float32 [1024, 640], P('batch', 'ctx')
- grad_w_gate_up: float32 [640, 4096], P('ctx', 'batch')
- grad_w_down: float32 [2048, 640], P('batch', 'ctx')
- grad_gains: float32 [3072], P(('batch', 'ctx'))
The draws below stay inside these ranges and needn't reach their ends.
Inputs may be any that keep to these rules, and one draw needn't show every extreme that they name: `block_order`: each block of 0 .. 15 appears once; slots 2c and 2c + 1 hold blocks b and 15 - b.
All inputs are finite; a program needn't handle non-finite values.
Results may differ from the reference program's by a relative error of at most 0.03.
Values may be sent and summed in bfloat16 or wider, within the bound.
A program may use at most 128 MiB of HBM per device.

```python
import jax
import jax.numpy as jnp
from jax import lax

D = 640
H = 4
HD = 256
FF = 2048
BLK = 64
SEQ_LEN = 1024
SEQUENCES = 16
QKV = 1536
GAINS = 3072
N_CTX = 8


def draw_block_order(key, part):
    key = jax.random.fold_in(key, 5)
    pair_key, flip_key = jax.random.split(key)
    early_ids = jax.random.permutation(pair_key, N_CTX).astype(jnp.int32)
    flip_bits = jax.random.randint(flip_key, (N_CTX,), 0, 2, dtype=jnp.int32)
    first_ids = jnp.where(flip_bits == 1, 2 * N_CTX - 1 - early_ids, early_ids)
    second = 2 * N_CTX - 1 - first_ids
    return jnp.stack([first_ids, second], axis=1).reshape(2 * N_CTX).astype(jnp.int32)


def steps_of(stream_key, shape, cuts, smallest, high):
    loudness, own = 1.0, jax.random.fold_in(stream_key, 6)
    for dim, shards_of in cuts:
        draws = jnp.exp(jax.random.uniform(jax.random.fold_in(own, dim), (shards_of,), jnp.float32, smallest / len(cuts), high / len(cuts)))
        loudness = loudness * jnp.repeat(draws, shape[dim] // shards_of).reshape([-1 if axis == dim else 1 for axis in range(len(shape))])
    return loudness


def centred(key, shape, deviation, most, cuts=(), kind=jnp.bfloat16):
    result = deviation * jax.random.normal(key, shape, jnp.float32)
    if cuts:
        result = result * steps_of(key, shape, cuts, -0.22, 0.18)
    return jnp.clip(result, -most, most).astype(kind)


def setup_inputs(seed: int = 0) -> dict:
    keys = jax.random.split(jax.random.key(seed), 9)
    tokens = centred(keys[0], (SEQUENCES, SEQ_LEN, D), 1.0, 6.0, ((0, 4), (1, 8)))
    w_qkv = centred(keys[1], (D, QKV), D ** -0.5, 0.25, ((0, 8), (1, 4)))
    w_out = centred(keys[2], (H * HD, D), (H * HD) ** -0.5, 0.1875, ((0, 4), (1, 8)))
    w_gate_up = centred(keys[3], (D, 2 * FF), D ** -0.5, 0.25, ((0, 8), (1, 4)))
    w_down = centred(keys[4], (FF, D), FF ** -0.5, 0.125, ((0, 4), (1, 8)))
    norm_gains = jnp.clip(jax.random.uniform(keys[5], (GAINS,), jnp.float32, -0.5, 0.5) * steps_of(keys[5], (GAINS,), ((0, 32),), -0.4, 0.0), -0.5, 0.5).astype(jnp.bfloat16)
    block_order = draw_block_order(jax.random.fold_in(keys[8], 71), 0)
    cotangent = centred(keys[7], (SEQUENCES, SEQ_LEN, D), 1.0, 6.0, ((0, 4), (1, 8)))
    return {"tokens": tokens, "w_qkv": w_qkv, "w_out": w_out, "w_gate_up": w_gate_up, "w_down": w_down, "norm_gains": norm_gains, "block_order": block_order, "cotangent": cotangent}


rope_base = 1000000.0
epsilon = 1e-06
neg_large = -1e+30

@jax.custom_vjp
def low(v):
    return lax.optimization_barrier(v.astype(jnp.bfloat16)).astype(jnp.float32)

@jax.custom_vjp
def low_back(v):
    return v

def low_keep(v):
    return (low(v), None)

def low_pass(kept, grad):
    return (grad,)

def back_keep(v):
    return (v, None)

def back_low(kept, grad):
    return (low(grad),)
low.defvjp(low_keep, low_pass)
low_back.defvjp(back_keep, back_low)

def rms_scale(values, gain_vec):
    mean_square = lax.optimization_barrier(jnp.mean(values * values, axis=-1, keepdims=True))
    return values * lax.rsqrt(mean_square + epsilon) * (1.0 + gain_vec)

def gelu_tanh(values):
    return 0.5 * values * (1.0 + jnp.tanh(0.7978845608028654 * (values + 0.044715 * values * values * values)))

def rope_tables(positions, head_size):
    half_size = head_size // 2
    exponent = jnp.arange(half_size, dtype=jnp.float32) * (2.0 / head_size)
    frequency = rope_base ** (-exponent)
    angles = positions.astype(jnp.float32)[:, None] * frequency[None, :]
    return (jnp.cos(angles), jnp.sin(angles))

def rotate(values, cosines, sine_vals):
    half_size = values.shape[-1] // 2
    first_half = values[..., :half_size]
    second_half = values[..., half_size:]
    return jnp.concatenate([first_half * cosines - second_half * sine_vals, second_half * cosines + first_half * sine_vals], axis=-1)

def layer_one(seq_tokens, w_qkv, w_out, w_gate_up, w_down, norm_gains, cosines, sine_vals, allowed):
    highest = lax.Precision.HIGHEST
    gain_in = norm_gains[0:D]
    gain_attn = norm_gains[D:2 * D]
    gain_pre = norm_gains[2 * D:3 * D]
    gain_post = norm_gains[3 * D:4 * D]
    gain_query = norm_gains[4 * D:4 * D + HD]
    gain_key = norm_gains[4 * D + HD:4 * D + 2 * HD]
    normed = low(rms_scale(seq_tokens, gain_in))
    projected = low_back(jnp.dot(normed, w_qkv, precision=highest))
    shaped = projected.reshape(projected.shape[0], H + 2, HD)
    queries = low(rotate(rms_scale(shaped[:, :H], gain_query), cosines[:, None, :], sine_vals[:, None, :]))
    key_vecs = low(rotate(rms_scale(shaped[:, H], gain_key), cosines, sine_vals))
    val_vecs = low(shaped[:, H + 1])
    score_scale = HD ** (-0.5)
    scores = low_back(jnp.einsum('lhd,md->hlm', queries, key_vecs, precision=highest) * score_scale)
    scores = jnp.where(allowed[None], scores, neg_large)
    row_max = lax.optimization_barrier(jnp.max(scores, axis=-1, keepdims=True))
    powers = jnp.exp(scores - row_max)
    soft_probs = powers / lax.optimization_barrier(jnp.sum(powers, axis=-1, keepdims=True))
    mixed_out = jnp.einsum('hlm,md->lhd', low(soft_probs), val_vecs, precision=highest)
    attended = low(low_back(mixed_out)).reshape(mixed_out.shape[0], H * HD)
    y_attn = low_back(jnp.dot(attended, w_out, precision=highest))
    residual = seq_tokens + rms_scale(y_attn, gain_attn)
    normed_two = low(rms_scale(residual, gain_pre))
    gate_up = low_back(jnp.dot(normed_two, w_gate_up, precision=highest))
    hidden = low(gelu_tanh(gate_up[:, :FF]) * gate_up[:, FF:])
    branch = low_back(jnp.dot(hidden, w_down, precision=highest))
    return residual + rms_scale(branch, gain_post)

def forward(tokens, w_qkv, w_out, w_gate_up, w_down, norm_gains, cosines, sine_vals, allowed):

    def one_sequence(seq_tokens):
        return layer_one(seq_tokens, w_qkv, w_out, w_gate_up, w_down, norm_gains, cosines, sine_vals, allowed)
    return lax.map(jax.checkpoint(one_sequence), tokens)

def reference(tokens, w_qkv, w_out, w_gate_up, w_down, norm_gains, block_order, cotangent):
    offsets = jnp.arange(BLK, dtype=jnp.int32)
    positions = (block_order.astype(jnp.int32)[:, None] * BLK + offsets[None, :]).reshape(-1)
    allowed = positions[None, :] <= positions[:, None]
    cosines, sine_vals = rope_tables(positions, HD)

    def wrapped(tok_float, qkv_float, out_float, gu_float, down_float, gain_float):
        return forward(tok_float, qkv_float, out_float, gu_float, down_float, gain_float, cosines, sine_vals, allowed)
    output, pull_back = jax.vjp(wrapped, tokens.astype(jnp.float32), w_qkv.astype(jnp.float32), w_out.astype(jnp.float32), w_gate_up.astype(jnp.float32), w_down.astype(jnp.float32), norm_gains.astype(jnp.float32))
    gradients = pull_back(cotangent.astype(jnp.float32))
    return (output.astype(jnp.bfloat16), gradients[0], gradients[1], gradients[2], gradients[3], gradients[4], gradients[5])
```

```python
import jax
import jax.numpy as jnp
from jax import lax
from jax.experimental import pallas as pl
from jax.experimental.pallas import tpu as pltpu
from jax.sharding import PartitionSpec as P

D = 640
H = 4
HD = 256
FF = 2048


rope_base = 1000000.0
epsilon = 1e-06
neg_large = -1e30


def rms_scale(values, gain_vec):
    mean_square = jnp.mean(values * values, axis=-1, keepdims=True)
    return values * lax.rsqrt(mean_square + epsilon) * (1.0 + gain_vec)


def gelu_tanh(values):
    return (
        0.5
        * values
        * (1.0 + jnp.tanh(0.7978845608028654 * (values + 0.044715 * values * values * values)))
    )


def rope_tables(positions, head_size):
    half_size = head_size // 2
    exponent = jnp.arange(half_size, dtype=jnp.float32) * (2.0 / head_size)
    frequency = rope_base ** (-exponent)
    angles = positions.astype(jnp.float32)[:, None] * frequency[None, :]
    return (jnp.cos(angles), jnp.sin(angles))


def rotate(values, cosines, sine_vals):
    half_size = values.shape[-1] // 2
    first_half = values[..., :half_size]
    second_half = values[..., half_size:]
    return jnp.concatenate(
        [
            first_half * cosines - second_half * sine_vals,
            second_half * cosines + first_half * sine_vals,
        ],
        axis=-1,
    )


def add_branch(branch, base_rows, gain_vec):
    return base_rows + rms_scale(branch, gain_vec)


def activate(gate_up):
    return gelu_tanh(gate_up[:, :FF]) * gate_up[:, FF:]


MESH = pl.DeviceIdType.MESH


def flip(index, bit):
    half = (index // bit) % 2
    return index + bit - 2 * bit * half


def greet(others):
    barrier = pltpu.get_barrier_semaphore()
    for other in others:
        pl.semaphore_signal(barrier, inc=1, device_id=other, device_id_type=MESH)
    pl.semaphore_wait(barrier, len(others))


def gather_kernel(chips, *refs):
    count = (len(refs) - 3) // 2
    shards, wholes = refs[:count], refs[count : 2 * count]
    own_sem, send_sem, recv_sem = refs[2 * count :]
    mine = lax.axis_index("batch")
    place = lax.axis_index("ctx")
    lane, chip = place % 2, place // 2
    mate = flip(place, 1)
    over_x, over_y = flip(mine, 1), flip(mine, 2)
    corner = flip(over_x, 2)
    line = [place] + [((chip + d) % chips) * 2 + lane for d in range(1, chips)]
    greet(
        [(mine, mate), (over_x, place), (over_y, place)] + [(mine, there) for there in line[1:]]
    )

    def window(which, row_owner, place_owner):
        whole = wholes[which]
        rows, width = shards[which].shape
        if which == 0:
            start = pl.multiple_of((row_owner * (2 * chips) + place_owner) * rows, rows)
            return whole.at[pl.ds(start, rows), :]
        return whole.at[
            pl.ds(pl.multiple_of(place_owner * rows, rows), rows),
            pl.ds(pl.multiple_of(row_owner * width, 128), width),
        ]

    sent = []
    used = [0] * count

    def send(which, row_owner, place_owner, target, source=None):
        copy = pltpu.make_async_remote_copy(
            src_ref=window(which, row_owner, place_owner) if source is None else source,
            dst_ref=window(which, row_owner, place_owner),
            send_sem=send_sem.at[which, used[which]],
            recv_sem=recv_sem.at[which, row_owner, place_owner],
            device_id=target,
            device_id_type=MESH,
        )
        used[which] += 1
        copy.start()
        sent.append(copy)

    def arrived(which, row_owner, place_owner):
        pltpu.make_async_copy(
            window(which, row_owner, place_owner),
            window(which, row_owner, place_owner),
            recv_sem.at[which, row_owner, place_owner],
        ).wait()

    first = [over_x] * (count - 1) + [over_y]
    second = [over_y] * (count - 1) + [over_x]
    own = []
    for which in range(count):
        copy = pltpu.make_async_copy(
            shards[which], window(which, mine, place), own_sem.at[which]
        )
        copy.start()
        own.append(copy)
        source = shards[which]
        for there in line[1:]:
            send(which, mine, place, (mine, there), source)
        send(which, mine, place, (first[which], place), source)
        send(which, mine, place, (second[which], place), source)
        send(which, mine, place, (mine, mate), source)
    for step in range(chips):
        for which in range(count):
            if step > 0:
                arrived(which, mine, line[step])
                send(which, mine, line[step], (first[which], place))
                send(which, mine, line[step], (second[which], place))
                send(which, mine, line[step], (mine, mate))
        for which in range(count):
            arrived(which, first[which], line[step])
            send(which, first[which], line[step], (second[which], place))
            send(which, first[which], line[step], (mine, mate))
    for step in range(chips):
        for which in range(count):
            arrived(which, second[which], line[step])
            send(which, second[which], line[step], (mine, mate))
        for which in range(count):
            arrived(which, corner, line[step])
            send(which, corner, line[step], (mine, mate))
    for step in range(chips):
        for which in range(count):
            for row_owner in (mine, over_x, over_y, corner):
                arrived(which, row_owner, flip(line[step], 1))
    for copy in own:
        copy.wait()
    for copy in sent:
        copy.wait_send()


def gather_weights(w_qkv, w_out, w_gate_up, w_down, norm_gains):
    groups, places = lax.axis_size("batch"), lax.axis_size("ctx")
    chips = places // 2
    rows = w_qkv.shape[0]
    if groups != 4 or rows % 16 != 0 or chips < 2:
        full = (
            lax.all_gather(lax.all_gather(w_qkv, "ctx", axis=0, tiled=True), "batch", axis=1, tiled=True),
            lax.all_gather(lax.all_gather(w_out, "ctx", axis=1, tiled=True), "batch", axis=0, tiled=True).T,
            lax.all_gather(lax.all_gather(w_gate_up, "ctx", axis=0, tiled=True), "batch", axis=1, tiled=True),
            lax.all_gather(lax.all_gather(w_down, "ctx", axis=1, tiled=True), "batch", axis=0, tiled=True).T,
            lax.all_gather(norm_gains, ("batch", "ctx"), axis=0, tiled=True),
        )
        return full
    gain_count = norm_gains.shape[0]
    gain_tile = jnp.pad(norm_gains[None, :], ((0, 15), (0, 128 - gain_count)))
    shards = (gain_tile, w_qkv, w_out.T, w_down.T, w_gate_up)
    shapes = [(groups * places * 16, 128)] + [
        (places * piece.shape[0], groups * piece.shape[1]) for piece in shards[1:]
    ]
    any_space = pl.BlockSpec(memory_space=pl.ANY)
    sends = 2 + chips + 2 * (chips - 1) + (4 * chips) + 2 * chips + 4
    gains, qkv, out_t, down_t, gate_up = pl.pallas_call(
        lambda *refs: gather_kernel(chips, *refs),
        out_shape=[jax.ShapeDtypeStruct(shape, jnp.bfloat16) for shape in shapes],
        in_specs=[any_space] * 5,
        out_specs=[any_space] * 5,
        scratch_shapes=[
            pltpu.SemaphoreType.DMA((5,)),
            pltpu.SemaphoreType.DMA((5, sends)),
            pltpu.SemaphoreType.DMA((5, groups, places)),
        ],
        compiler_params=pltpu.CompilerParams(collective_id=0, has_side_effects=True),
        name="gather_weights",
    )(*shards)
    gains = gains.reshape(groups * places, 16, 128)[:, 0, :gain_count].reshape(-1)
    return qkv, out_t, gate_up, down_t, gains


def body(tokens, w_qkv, w_out, w_gate_up, w_down, norm_gains, block_order, cotangent):
    seq_count, tok_rows, _ = tokens.shape
    block_len = tok_rows // 2
    ctx_index = lax.axis_index("ctx")
    score_scale = HD ** (-0.5)
    full_qkv, full_out, full_gu, full_down, full_gains = gather_weights(
        w_qkv, w_out, w_gate_up, w_down, norm_gains
    )
    gain_all = full_gains.astype(jnp.float32)
    gain_in = gain_all[0:D]
    gain_attn = gain_all[D : 2 * D]
    gain_pre = gain_all[2 * D : 3 * D]
    gain_post = gain_all[3 * D : 4 * D]
    gain_query = gain_all[4 * D : 4 * D + HD]
    gain_key = gain_all[4 * D + HD : 4 * D + 2 * HD]
    offsets = jnp.arange(block_len, dtype=jnp.int32)
    key_pos = (block_order[:, None] * block_len + offsets[None, :]).reshape(-1)
    query_pos = lax.dynamic_slice_in_dim(key_pos, ctx_index * tok_rows, tok_rows)
    cosines, sine_vals = rope_tables(query_pos, HD)
    flat = tokens.reshape(seq_count * tok_rows, D).astype(jnp.float32)
    normed, back_one = jax.vjp(rms_scale, flat, gain_in)
    normed_b = normed.astype(jnp.bfloat16)
    projected = jnp.dot(normed_b, full_qkv, preferred_element_type=jnp.float32)

    def prepare(raw_proj, gain_q, gain_k):
        shaped = raw_proj.reshape(seq_count, tok_rows, H + 2, HD)
        queries = rotate(
            rms_scale(shaped[:, :, :H], gain_q),
            cosines[None, :, None, :],
            sine_vals[None, :, None, :],
        )
        key_vecs = rotate(rms_scale(shaped[:, :, H], gain_k), cosines[None], sine_vals[None])
        return (queries.transpose(0, 2, 1, 3), key_vecs, shaped[:, :, H + 1])

    (queries, key_vecs, val_vecs), back_prep = jax.vjp(prepare, projected, gain_query, gain_key)
    query_b = queries.astype(jnp.bfloat16)
    key_b = key_vecs.astype(jnp.bfloat16)
    value_b = val_vecs.astype(jnp.bfloat16)

    key_value = lax.all_gather(
        jnp.concatenate([key_b, value_b], axis=-1), "ctx", axis=1, tiled=True
    )
    key_piece, value_piece = key_value[..., :HD], key_value[..., HD:]
    allowed = key_pos[None, :] <= query_pos[:, None]
    raw_scores = (
        jnp.einsum("shrd,snd->shrn", query_b, key_piece, preferred_element_type=jnp.float32)
        * score_scale
    )
    scores = jnp.where(allowed, raw_scores, neg_large)
    row_max = jnp.max(scores, axis=-1, keepdims=True)
    powers = jnp.exp(scores - row_max)
    soft_b = (powers / jnp.sum(powers, axis=-1, keepdims=True)).astype(jnp.bfloat16)
    attn_out = jnp.einsum(
        "shrn,snd->shrd", soft_b, value_piece, preferred_element_type=jnp.float32
    )
    attn_b = (
        attn_out.transpose(0, 2, 1, 3).reshape(seq_count * tok_rows, H * HD).astype(jnp.bfloat16)
    )
    y_attn = jnp.einsum("te,de->td", attn_b, full_out, preferred_element_type=jnp.float32)
    residual, back_attn = jax.vjp(add_branch, y_attn, flat, gain_attn)
    normed_two, back_two = jax.vjp(rms_scale, residual, gain_pre)
    normed_two_b = normed_two.astype(jnp.bfloat16)
    gate_up = jnp.dot(normed_two_b, full_gu, preferred_element_type=jnp.float32)
    hidden, back_act = jax.vjp(activate, gate_up)
    hidden_b = hidden.astype(jnp.bfloat16)
    branch = jnp.einsum("tf,df->td", hidden_b, full_down, preferred_element_type=jnp.float32)
    output, back_out = jax.vjp(add_branch, branch, residual, gain_post)
    result = output.astype(jnp.bfloat16).reshape(tokens.shape)
    seed_grad = cotangent.reshape(seq_count * tok_rows, D).astype(jnp.float32)
    d_branch, d_resid_a, d_gain_post = back_out(seed_grad)
    d_branch_b = d_branch.astype(jnp.bfloat16)
    grad_down = jnp.einsum("tf,td->fd", hidden_b, d_branch_b, preferred_element_type=jnp.float32)
    d_hidden = jnp.einsum("td,df->tf", d_branch_b, full_down, preferred_element_type=jnp.float32)
    (d_gate_up,) = back_act(d_hidden)
    d_gate_up_b = d_gate_up.astype(jnp.bfloat16)
    grad_gu = jnp.einsum("td,tf->df", normed_two_b, d_gate_up_b, preferred_element_type=jnp.float32)
    d_normed_two = jnp.einsum("tf,df->td", d_gate_up_b, full_gu, preferred_element_type=jnp.float32)
    d_resid_b, d_gain_pre = back_two(d_normed_two)
    d_y_attn, d_flat_a, d_gain_attn = back_attn(d_resid_a + d_resid_b)
    d_y_attn_b = d_y_attn.astype(jnp.bfloat16)
    grad_out = jnp.einsum("te,td->ed", attn_b, d_y_attn_b, preferred_element_type=jnp.float32)
    d_attn_rows = jnp.einsum(
        "td,de->te", d_y_attn_b, full_out, preferred_element_type=jnp.float32
    ).astype(jnp.bfloat16)
    d_attn = d_attn_rows.reshape(seq_count, tok_rows, H, HD).transpose(0, 2, 1, 3)
    row_dot = jnp.sum(d_attn.astype(jnp.float32) * attn_out, axis=-1)

    d_probs = jnp.einsum(
        "shrd,snd->shrn", d_attn, value_piece, preferred_element_type=jnp.float32
    )
    d_scores = (soft_b.astype(jnp.float32) * (d_probs - row_dot[..., None])).astype(jnp.bfloat16)
    d_key = (
        jnp.einsum("shrn,shrd->snd", d_scores, query_b, preferred_element_type=jnp.float32)
        * score_scale
    )
    d_value = jnp.einsum("shrn,shrd->snd", soft_b, d_attn, preferred_element_type=jnp.float32)
    d_key_value = lax.psum_scatter(
        jnp.concatenate([d_key, d_value], axis=-1).astype(jnp.bfloat16),
        "ctx",
        scatter_dimension=1,
        tiled=True,
    ).astype(jnp.float32)
    grad_key, grad_value = d_key_value[..., :HD], d_key_value[..., HD:]
    grad_query = (
        jnp.einsum("shrn,snd->shrd", d_scores, key_piece, preferred_element_type=jnp.float32)
        * score_scale
    )
    d_projected, d_gain_query, d_gain_key = back_prep((grad_query, grad_key, grad_value))
    d_projected_b = d_projected.astype(jnp.bfloat16)
    grad_qkv = jnp.einsum("td,te->de", normed_b, d_projected_b, preferred_element_type=jnp.float32)
    d_normed = jnp.einsum("te,de->td", d_projected_b, full_qkv, preferred_element_type=jnp.float32)
    d_flat_b, d_gain_in = back_one(d_normed)
    grad_tokens = (d_flat_a + d_flat_b).reshape(tokens.shape)
    grad_gain_all = jnp.concatenate(
        [d_gain_in, d_gain_attn, d_gain_pre, d_gain_post, d_gain_query, d_gain_key]
    )
    batch_sums = (
        lax.psum_scatter(
            grad_qkv.astype(jnp.bfloat16), "batch", scatter_dimension=1, tiled=True
        ).astype(jnp.float32),
        lax.psum_scatter(
            grad_out.astype(jnp.bfloat16), "batch", scatter_dimension=0, tiled=True
        ).astype(jnp.float32),
        lax.psum_scatter(
            grad_gu.astype(jnp.bfloat16), "batch", scatter_dimension=1, tiled=True
        ).astype(jnp.float32),
        lax.psum_scatter(
            grad_down.astype(jnp.bfloat16), "batch", scatter_dimension=0, tiled=True
        ).astype(jnp.float32),
        lax.psum_scatter(
            grad_gain_all.astype(jnp.bfloat16), "batch", scatter_dimension=0, tiled=True
        ).astype(jnp.float32),
    )
    sum_qkv, sum_out, sum_gu, sum_down, sum_gains = batch_sums
    final_qkv, final_out, final_gu, final_down, final_gains = (
        lax.psum_scatter(
            sum_qkv.astype(jnp.bfloat16), "ctx", scatter_dimension=0, tiled=True
        ).astype(jnp.float32),
        lax.psum_scatter(
            sum_out.astype(jnp.bfloat16), "ctx", scatter_dimension=1, tiled=True
        ).astype(jnp.float32),
        lax.psum_scatter(
            sum_gu.astype(jnp.bfloat16), "ctx", scatter_dimension=0, tiled=True
        ).astype(jnp.float32),
        lax.psum_scatter(
            sum_down.astype(jnp.bfloat16), "ctx", scatter_dimension=1, tiled=True
        ).astype(jnp.float32),
        lax.psum_scatter(
            sum_gains.astype(jnp.bfloat16), "ctx", scatter_dimension=0, tiled=True
        ).astype(jnp.float32),
    )
    return (result, grad_tokens, final_qkv, final_out, final_gu, final_down, final_gains)


def solution(mesh):
    in_specs = (
        P("batch", "ctx", None),
        P("ctx", "batch"),
        P("batch", "ctx"),
        P("ctx", "batch"),
        P("batch", "ctx"),
        P(("batch", "ctx")),
        P(),
        P("batch", "ctx", None),
    )
    out_specs = (
        P("batch", "ctx", None),
        P("batch", "ctx", None),
        P("ctx", "batch"),
        P("batch", "ctx"),
        P("ctx", "batch"),
        P("batch", "ctx"),
        P(("batch", "ctx")),
    )
    return jax.shard_map(body, mesh=mesh, in_specs=in_specs, out_specs=out_specs, check_vma=False)
```

```python
import jax
import jax.numpy as jnp
from jax import lax
from jax.experimental import pallas as pl
from jax.experimental.pallas import tpu as pltpu
from jax.sharding import PartitionSpec as P

D = 640
H = 4
HD = 256
FF = 2048


rope_base = 1000000.0
epsilon = 1e-06
neg_large = -1e30


def rms_scale(values, gain_vec):
    mean_square = jnp.mean(values * values, axis=-1, keepdims=True)
    return values * lax.rsqrt(mean_square + epsilon) * (1.0 + gain_vec)


def gelu_tanh(values):
    return (
        0.5
        * values
        * (1.0 + jnp.tanh(0.7978845608028654 * (values + 0.044715 * values * values * values)))
    )


def rope_tables(positions, head_size):
    half_size = head_size // 2
    exponent = jnp.arange(half_size, dtype=jnp.float32) * (2.0 / head_size)
    frequency = rope_base ** (-exponent)
    angles = positions.astype(jnp.float32)[:, None] * frequency[None, :]
    return (jnp.cos(angles), jnp.sin(angles))


def rotate(values, cosines, sine_vals):
    half_size = values.shape[-1] // 2
    first_half = values[..., :half_size]
    second_half = values[..., half_size:]
    return jnp.concatenate(
        [
            first_half * cosines - second_half * sine_vals,
            second_half * cosines + first_half * sine_vals,
        ],
        axis=-1,
    )


def add_branch(branch, base_rows, gain_vec):
    return base_rows + rms_scale(branch, gain_vec)


def activate(gate_up):
    return gelu_tanh(gate_up[:, :FF]) * gate_up[:, FF:]


MESH = pl.DeviceIdType.MESH


def flip(index, bit):
    half = (index // bit) % 2
    return index + bit - 2 * bit * half


def greet(others):
    barrier = pltpu.get_barrier_semaphore()
    for other in others:
        pl.semaphore_signal(barrier, inc=1, device_id=other, device_id_type=MESH)
    pl.semaphore_wait(barrier, len(others))


def gather_kernel(chips, y_first, stacked, with_rows, *refs):
    count = len(y_first)
    shards, refs = refs[:count], refs[count:]
    if with_rows:
        row_shard, refs = refs[0], refs[1:]
    wholes, refs = refs[:count], refs[count:]
    if with_rows:
        row_whole, refs = refs[0], refs[1:]
    own_sem, send_sem, recv_sem = refs[:3]
    mine = lax.axis_index("batch")
    place = lax.axis_index("ctx")
    lane, chip = place % 2, place // 2
    mate = flip(place, 1)
    over_x, over_y = flip(mine, 1), flip(mine, 2)
    corner = flip(over_x, 2)
    line = [place] + [((chip + d) % chips) * 2 + lane for d in range(1, chips)]
    greet(
        [(mine, mate), (over_x, place), (over_y, place)] + [(mine, there) for there in line[1:]]
    )

    def window(which, row_owner, place_owner):
        whole = wholes[which]
        rows, width = shards[which].shape
        if stacked[which]:
            start = pl.multiple_of((row_owner * (2 * chips) + place_owner) * rows, rows)
            return whole.at[pl.ds(start, rows), :]
        return whole.at[
            pl.ds(pl.multiple_of(place_owner * rows, rows), rows),
            pl.ds(pl.multiple_of(row_owner * width, 128), width),
        ]

    sent = []
    used = [0] * count

    def send(which, row_owner, place_owner, target, source=None):
        copy = pltpu.make_async_remote_copy(
            src_ref=window(which, row_owner, place_owner) if source is None else source,
            dst_ref=window(which, row_owner, place_owner),
            send_sem=send_sem.at[which, used[which]],
            recv_sem=recv_sem.at[which, row_owner, place_owner],
            device_id=target,
            device_id_type=MESH,
        )
        used[which] += 1
        copy.start()
        sent.append(copy)

    def arrived(which, row_owner, place_owner):
        pltpu.make_async_copy(
            window(which, row_owner, place_owner),
            window(which, row_owner, place_owner),
            recv_sem.at[which, row_owner, place_owner],
        ).wait()

    first = [over_y if y else over_x for y in y_first]
    second = [over_x if y else over_y for y in y_first]
    own = []
    for which in range(count):
        copy = pltpu.make_async_copy(
            shards[which], window(which, mine, place), own_sem.at[which]
        )
        copy.start()
        own.append(copy)
        source = shards[which]
        for there in line[1:]:
            send(which, mine, place, (mine, there), source)
        send(which, mine, place, (first[which], place), source)
        send(which, mine, place, (second[which], place), source)
        send(which, mine, place, (mine, mate), source)
    if with_rows:
        rows_own_sem, rows_send_sem, rows_recv_sem = refs[3:]
        row_count = row_shard.shape[1]

        def row_window(owner):
            start = pl.multiple_of(owner * row_count, row_count)
            return row_whole.at[:, pl.ds(start, row_count), :]

        def send_rows(slot, owner, target, source):
            copy = pltpu.make_async_remote_copy(
                src_ref=source,
                dst_ref=row_window(owner),
                send_sem=rows_send_sem.at[slot],
                recv_sem=rows_recv_sem.at[owner],
                device_id=(mine, target),
                device_id_type=MESH,
            )
            copy.start()
            sent.append(copy)

        def rows_arrived(owner):
            pltpu.make_async_copy(
                row_window(owner), row_window(owner), rows_recv_sem.at[owner]
            ).wait()

        copy = pltpu.make_async_copy(row_shard, row_window(place), rows_own_sem)
        copy.start()
        own.append(copy)
        for step in range(1, chips):
            send_rows(step - 1, place, line[step], row_shard)
        send_rows(chips - 1, place, mate, row_shard)
    for step in range(chips):
        for which in range(count):
            if step > 0:
                arrived(which, mine, line[step])
                send(which, mine, line[step], (first[which], place))
                send(which, mine, line[step], (second[which], place))
                send(which, mine, line[step], (mine, mate))
        for which in range(count):
            arrived(which, first[which], line[step])
            send(which, first[which], line[step], (second[which], place))
            send(which, first[which], line[step], (mine, mate))
    for step in range(chips):
        for which in range(count):
            arrived(which, second[which], line[step])
            send(which, second[which], line[step], (mine, mate))
        for which in range(count):
            arrived(which, corner, line[step])
            send(which, corner, line[step], (mine, mate))
    if with_rows:
        for step in range(1, chips):
            rows_arrived(line[step])
            send_rows(chips - 1 + step, line[step], mate, row_window(line[step]))
        for step in range(chips):
            rows_arrived(flip(line[step], 1))
    for step in range(chips):
        for which in range(count):
            for row_owner in (mine, over_x, over_y, corner):
                arrived(which, row_owner, flip(line[step], 1))
    for copy in own:
        copy.wait()
    for copy in sent:
        copy.wait_send()


def gather(shards, y_first, stacked, rows, collective_id, name):
    groups, places = lax.axis_size("batch"), lax.axis_size("ctx")
    chips = places // 2
    count = len(shards)
    shapes = [
        (groups * places * piece.shape[0], piece.shape[1])
        if under
        else (places * piece.shape[0], groups * piece.shape[1])
        for piece, under in zip(shards, stacked)
    ]
    operands = list(shards)
    scratch = [
        pltpu.SemaphoreType.DMA((count,)),
        pltpu.SemaphoreType.DMA((count, 8 * chips)),
        pltpu.SemaphoreType.DMA((count, groups, places)),
    ]
    if rows is not None:
        operands.append(rows)
        shapes.append((rows.shape[0], places * rows.shape[1], rows.shape[2]))
        scratch += [
            pltpu.SemaphoreType.DMA(()),
            pltpu.SemaphoreType.DMA((2 * chips,)),
            pltpu.SemaphoreType.DMA((places,)),
        ]
    any_space = pl.BlockSpec(memory_space=pl.ANY)
    return pl.pallas_call(
        lambda *refs: gather_kernel(chips, y_first, stacked, rows is not None, *refs),
        out_shape=[jax.ShapeDtypeStruct(shape, jnp.bfloat16) for shape in shapes],
        in_specs=[any_space] * len(operands),
        out_specs=[any_space] * len(operands),
        scratch_shapes=scratch,
        compiler_params=pltpu.CompilerParams(collective_id=collective_id, has_side_effects=True),
        name=name,
    )(*operands)


def scatter_kernel(chips, y_first, with_rows, *refs):
    count = len(y_first)
    total = count + (1 if with_rows else 0)
    terms, refs = refs[:total], refs[total:]
    outs, refs = refs[:total], refs[total:]
    held, refs = refs[:total], refs[total:]
    got_mate, refs = refs[:total], refs[total:]
    got_first, refs = refs[:count], refs[count:]
    got_second, refs = refs[:count], refs[count:]
    got_line, refs = refs[:total], refs[total:]
    own_sem, mate_sem, first_sem, second_sem, line_sem = refs
    mine = lax.axis_index("batch")
    place = lax.axis_index("ctx")
    lane, chip = place % 2, place // 2
    mate = flip(place, 1)
    over_x, over_y = flip(mine, 1), flip(mine, 2)
    first = [over_y if y else over_x for y in y_first]
    second = [over_x if y else over_y for y in y_first]
    bit = [1 if y else 2 for y in y_first]
    chips_at = [chip] + [(chip + d) % chips for d in range(1, chips)]
    greet(
        [(mine, mate), (over_x, place), (over_y, place)]
        + [(mine, there * 2 + lane) for there in chips_at[1:]]
    )
    sent = []

    def send(source, target, sems, slot, device):
        copy = pltpu.make_async_remote_copy(
            src_ref=source,
            dst_ref=target,
            send_sem=sems.at[(0, *slot)],
            recv_sem=sems.at[(1, *slot)],
            device_id=device,
            device_id_type=MESH,
        )
        copy.start()
        sent.append(copy)

    def arrived(target, sems, slot):
        pltpu.make_async_copy(target, target, sems.at[(1, *slot)]).wait()

    def part(which, owner):
        if which == count:
            rows = outs[which].shape[1]
            return terms[which].at[:, pl.ds(pl.multiple_of(owner * rows, rows), rows), :]
        rows = outs[which].shape[0]
        return terms[which].at[pl.ds(pl.multiple_of(owner * rows, rows), rows), :]

    def in_groups(which, step):
        if which == count:
            pl.loop(0, outs[which].shape[0])(lambda i: step((i,)))
            return
        rows = outs[which].shape[0]
        group = 16 if rows % 16 == 0 else rows
        pl.loop(0, rows // group)(
            lambda i: step((pl.ds(pl.multiple_of(i * group, group), group),))
        )

    def columns(which, owner):
        width = outs[which].shape[1]
        return pl.ds(pl.multiple_of(owner * width, 128), width)

    order = list(range(1, chips)) + [0]
    own = {}
    whiches = ([count] if with_rows else []) + list(range(count))
    for d in order:
        for which in whiches:
            there = chips_at[d]
            send(
                part(which, there * 2 + 1 - lane),
                got_mate[which].at[there],
                mate_sem,
                (which, there),
                (mine, mate),
            )
            copy = pltpu.make_async_copy(
                part(which, there * 2 + lane), held[which].at[d], own_sem.at[which, d]
            )
            copy.start()
            own[which, d] = copy

    f32 = jnp.float32
    for d in order:
        there = chips_at[d]
        for which in whiches:
            arrived(got_mate[which].at[there], mate_sem, (which, there))
            own[which, d].wait()

            def add_mate(spot, which=which, there=there, d=d):
                at = (there, *spot)
                got_mate[which][at] = (
                    got_mate[which][at].astype(f32) + held[which][(d, *spot)].astype(f32)
                ).astype(got_mate[which].dtype)

            in_groups(which, add_mate)
            if which == count:
                if d > 0:
                    send(
                        got_mate[which].at[there],
                        got_line[which].at[d - 1],
                        line_sem,
                        (which, d - 1),
                        (mine, there * 2 + lane),
                    )
                continue
            for slot, owner in ((1, flip(first[which], bit[which])), (0, first[which])):
                send(
                    got_mate[which].at[there, :, columns(which, owner)],
                    got_first[which].at[there, slot],
                    first_sem,
                    (which, there, slot),
                    (first[which], place),
                )
    for d in order:
        there = chips_at[d]
        for which in range(count):
            for slot, owner in ((1, second[which]), (0, mine)):
                arrived(got_first[which].at[there, slot], first_sem, (which, there, slot))

                def add_first(spot, which=which, there=there, slot=slot, owner=owner):
                    at = (there, slot, *spot)
                    got_first[which][at] = (
                        got_first[which][at].astype(f32)
                        + got_mate[which][(there, *spot, columns(which, owner))].astype(f32)
                    ).astype(got_first[which].dtype)

                in_groups(which, add_first)
                if slot == 1:
                    send(
                        got_first[which].at[there, 1],
                        got_second[which].at[there],
                        second_sem,
                        (which, there),
                        (second[which], place),
                    )
    for d in order:
        there = chips_at[d]
        for which in range(count):
            arrived(got_second[which].at[there], second_sem, (which, there))
            if d == 0:
                continue

            def add_second(spot, which=which, there=there):
                at = (there, *spot)
                got_second[which][at] = (
                    got_second[which][at].astype(f32)
                    + got_first[which][(there, 0, *spot)].astype(f32)
                ).astype(got_second[which].dtype)

            in_groups(which, add_second)
            send(
                got_second[which].at[there],
                got_line[which].at[d - 1],
                line_sem,
                (which, d - 1),
                (mine, there * 2 + lane),
            )
    for which in whiches:
        for d in range(1, chips):
            arrived(got_line[which].at[d - 1], line_sem, (which, d - 1))

        def finish(spot, which=which):
            if which == count:
                value = got_mate[which][(chip, *spot)].astype(f32)
            else:
                value = got_second[which][(chip, *spot)].astype(f32)
                value = value + got_first[which][(chip, 0, *spot)].astype(f32)
            for d in range(1, chips):
                value = value + got_line[which][(d - 1, *spot)].astype(f32)
            outs[which][spot] = value

        in_groups(which, finish)
    for copy in sent:
        copy.wait_send()


def scatter(terms, y_first, rows, collective_id, name):
    groups, places = lax.axis_size("batch"), lax.axis_size("ctx")
    chips = places // 2
    pieces = [(term.shape[0] // places, term.shape[1] // groups) for term in terms]
    kinds = [term.dtype for term in terms]
    operands = list(terms)
    outs = list(pieces)
    wide = [(chips, piece[0], groups * piece[1]) for piece in pieces]
    if rows is not None:
        piece = (rows.shape[0], rows.shape[1] // places, rows.shape[2])
        operands.append(rows)
        outs.append(piece)
        wide.append((chips, *piece))
        kinds.append(rows.dtype)
    count, total = len(terms), len(operands)
    scratch = [pltpu.VMEM(shape, kind) for shape, kind in zip(wide, kinds)] * 2
    scratch += [pltpu.VMEM((chips, 2, *piece), kind) for piece, kind in zip(pieces, kinds)]
    scratch += [pltpu.VMEM((chips, *piece), kind) for piece, kind in zip(pieces, kinds)]
    scratch += [pltpu.VMEM((chips - 1, *piece), kind) for piece, kind in zip(outs, kinds)]
    scratch += [
        pltpu.SemaphoreType.DMA((total, chips)),
        pltpu.SemaphoreType.DMA((2, total, chips)),
        pltpu.SemaphoreType.DMA((2, count, chips, 2)),
        pltpu.SemaphoreType.DMA((2, count, chips)),
        pltpu.SemaphoreType.DMA((2, total, chips - 1)),
    ]
    return pl.pallas_call(
        lambda *refs: scatter_kernel(chips, y_first, rows is not None, *refs),
        out_shape=[jax.ShapeDtypeStruct(shape, jnp.float32) for shape in outs],
        in_specs=[pl.BlockSpec(memory_space=pl.ANY)] * total,
        out_specs=[pl.BlockSpec(memory_space=pltpu.VMEM)] * total,
        scratch_shapes=scratch,
        compiler_params=pltpu.CompilerParams(
            collective_id=collective_id, has_side_effects=True, vmem_limit_bytes=40 * 2**20
        ),
        name=name,
    )(*operands)


def fits_kernels(w_qkv):
    groups, places = lax.axis_size("batch"), lax.axis_size("ctx")
    return groups == 4 and places >= 4 and w_qkv.shape[0] % 16 == 0


def gather_all(value, ctx_dim):
    part = lax.all_gather(value, "ctx", axis=ctx_dim, tiled=True)
    return lax.all_gather(part, "batch", axis=1 - ctx_dim, tiled=True)


def scatter_all(value):
    part = lax.psum_scatter(
        value.astype(jnp.bfloat16), "batch", scatter_dimension=1, tiled=True
    )
    return lax.psum_scatter(part, "ctx", scatter_dimension=0, tiled=True).astype(jnp.float32)


def body(tokens, w_qkv, w_out, w_gate_up, w_down, norm_gains, block_order, cotangent):
    seq_count, tok_rows, _ = tokens.shape
    block_len = tok_rows // 2
    ctx_index = lax.axis_index("ctx")
    score_scale = HD ** (-0.5)
    kernels = fits_kernels(w_qkv)
    group_count, ctx_size = lax.axis_size("batch"), lax.axis_size("ctx")
    device_count = group_count * ctx_size
    gain_count = norm_gains.shape[0]
    if kernels:
        gain_tile = jnp.pad(norm_gains[None, :], ((0, 15), (0, 128 - gain_count)))
        gain_tiles, full_qkv = gather(
            (gain_tile, w_qkv), (True, False), (True, False), None, 0, "gather_qkv"
        )
        full_gains = gain_tiles.reshape(device_count, 16, 128)[:, 0, :gain_count].reshape(-1)
    else:
        full_qkv = gather_all(w_qkv, 0)
        full_gains = lax.all_gather(norm_gains, ("batch", "ctx"), axis=0, tiled=True)
    gain_all = full_gains.astype(jnp.float32)
    gain_in = gain_all[0:D]
    gain_attn = gain_all[D : 2 * D]
    gain_pre = gain_all[2 * D : 3 * D]
    gain_post = gain_all[3 * D : 4 * D]
    gain_query = gain_all[4 * D : 4 * D + HD]
    gain_key = gain_all[4 * D + HD : 4 * D + 2 * HD]
    offsets = jnp.arange(block_len, dtype=jnp.int32)
    key_pos = (block_order[:, None] * block_len + offsets[None, :]).reshape(-1)
    query_pos = lax.dynamic_slice_in_dim(key_pos, ctx_index * tok_rows, tok_rows)
    cosines, sine_vals = rope_tables(query_pos, HD)
    flat = tokens.reshape(seq_count * tok_rows, D).astype(jnp.float32)
    normed, back_one = jax.vjp(rms_scale, flat, gain_in)
    normed_b = normed.astype(jnp.bfloat16)
    projected = jnp.dot(normed_b, full_qkv, preferred_element_type=jnp.float32)

    def prepare(raw_proj, gain_q, gain_k):
        shaped = raw_proj.reshape(seq_count, tok_rows, H + 2, HD)
        queries = rotate(
            rms_scale(shaped[:, :, :H], gain_q),
            cosines[None, :, None, :],
            sine_vals[None, :, None, :],
        )
        key_vecs = rotate(rms_scale(shaped[:, :, H], gain_k), cosines[None], sine_vals[None])
        return (queries.transpose(0, 2, 1, 3), key_vecs, shaped[:, :, H + 1])

    (queries, key_vecs, val_vecs), back_prep = jax.vjp(prepare, projected, gain_query, gain_key)
    query_b = queries.astype(jnp.bfloat16)
    key_b = key_vecs.astype(jnp.bfloat16)
    value_b = val_vecs.astype(jnp.bfloat16)

    key_value_own = jnp.concatenate([key_b, value_b], axis=-1)
    if kernels:
        full_out, full_down, full_gu, key_value = gather(
            (w_out.T, w_down.T, w_gate_up),
            (False, False, True),
            (False, False, False),
            key_value_own,
            1,
            "gather_rest",
        )
    else:
        full_out = gather_all(w_out, 1).T
        full_down = gather_all(w_down, 1).T
        full_gu = gather_all(w_gate_up, 0)
        key_value = lax.all_gather(key_value_own, "ctx", axis=1, tiled=True)
    key_piece, value_piece = key_value[..., :HD], key_value[..., HD:]
    allowed = key_pos[None, :] <= query_pos[:, None]
    raw_scores = (
        jnp.einsum("shrd,snd->shrn", query_b, key_piece, preferred_element_type=jnp.float32)
        * score_scale
    )
    scores = jnp.where(allowed, raw_scores, neg_large)
    row_max = jnp.max(scores, axis=-1, keepdims=True)
    powers = jnp.exp(scores - row_max)
    soft_b = (powers / jnp.sum(powers, axis=-1, keepdims=True)).astype(jnp.bfloat16)
    attn_out = jnp.einsum(
        "shrn,snd->shrd", soft_b, value_piece, preferred_element_type=jnp.float32
    )
    attn_b = (
        attn_out.transpose(0, 2, 1, 3).reshape(seq_count * tok_rows, H * HD).astype(jnp.bfloat16)
    )
    y_attn = jnp.einsum("te,de->td", attn_b, full_out, preferred_element_type=jnp.float32)
    residual, back_attn = jax.vjp(add_branch, y_attn, flat, gain_attn)
    normed_two, back_two = jax.vjp(rms_scale, residual, gain_pre)
    normed_two_b = normed_two.astype(jnp.bfloat16)
    gate_up = jnp.dot(normed_two_b, full_gu, preferred_element_type=jnp.float32)
    hidden, back_act = jax.vjp(activate, gate_up)
    hidden_b = hidden.astype(jnp.bfloat16)
    branch = jnp.einsum("tf,df->td", hidden_b, full_down, preferred_element_type=jnp.float32)
    output, back_out = jax.vjp(add_branch, branch, residual, gain_post)
    result = output.astype(jnp.bfloat16).reshape(tokens.shape)
    seed_grad = cotangent.reshape(seq_count * tok_rows, D).astype(jnp.float32)
    d_branch, d_resid_a, d_gain_post = back_out(seed_grad)
    d_branch_b = d_branch.astype(jnp.bfloat16)
    grad_down = jnp.einsum("td,tf->df", d_branch_b, hidden_b, preferred_element_type=jnp.float32)
    d_hidden = jnp.einsum("td,df->tf", d_branch_b, full_down, preferred_element_type=jnp.float32)
    (d_gate_up,) = back_act(d_hidden)
    d_gate_up_b = d_gate_up.astype(jnp.bfloat16)
    grad_gu = jnp.einsum("td,tf->df", normed_two_b, d_gate_up_b, preferred_element_type=jnp.float32)
    d_normed_two = jnp.einsum("tf,df->td", d_gate_up_b, full_gu, preferred_element_type=jnp.float32)
    d_resid_b, d_gain_pre = back_two(d_normed_two)
    d_y_attn, d_flat_a, d_gain_attn = back_attn(d_resid_a + d_resid_b)
    d_y_attn_b = d_y_attn.astype(jnp.bfloat16)
    grad_out = jnp.einsum("td,te->de", d_y_attn_b, attn_b, preferred_element_type=jnp.float32)
    d_attn_rows = jnp.einsum(
        "td,de->te", d_y_attn_b, full_out, preferred_element_type=jnp.float32
    ).astype(jnp.bfloat16)
    d_attn = d_attn_rows.reshape(seq_count, tok_rows, H, HD).transpose(0, 2, 1, 3)
    row_dot = jnp.sum(d_attn.astype(jnp.float32) * attn_out, axis=-1)

    d_probs = jnp.einsum(
        "shrd,snd->shrn", d_attn, value_piece, preferred_element_type=jnp.float32
    )
    d_scores = (soft_b.astype(jnp.float32) * (d_probs - row_dot[..., None])).astype(jnp.bfloat16)
    d_key = (
        jnp.einsum("shrn,shrd->snd", d_scores, query_b, preferred_element_type=jnp.float32)
        * score_scale
    )
    d_value = jnp.einsum("shrn,shrd->snd", soft_b, d_attn, preferred_element_type=jnp.float32)
    d_key_value_all = jnp.concatenate([d_key, d_value], axis=-1).astype(jnp.bfloat16)
    if kernels:
        final_out, final_down, final_gu, d_key_value = scatter(
            (
                grad_out.astype(jnp.bfloat16),
                grad_down.astype(jnp.bfloat16),
                grad_gu.astype(jnp.bfloat16),
            ),
            (True, True, False),
            d_key_value_all,
            2,
            "scatter_rest",
        )
    else:
        final_out, final_down, final_gu = (
            scatter_all(grad_out),
            scatter_all(grad_down),
            scatter_all(grad_gu),
        )
        d_key_value = lax.psum_scatter(
            d_key_value_all, "ctx", scatter_dimension=1, tiled=True
        ).astype(jnp.float32)
    grad_key, grad_value = d_key_value[..., :HD], d_key_value[..., HD:]
    grad_query = (
        jnp.einsum("shrn,snd->shrd", d_scores, key_piece, preferred_element_type=jnp.float32)
        * score_scale
    )
    d_projected, d_gain_query, d_gain_key = back_prep((grad_query, grad_key, grad_value))
    d_projected_b = d_projected.astype(jnp.bfloat16)
    grad_qkv = jnp.einsum("td,te->de", normed_b, d_projected_b, preferred_element_type=jnp.float32)
    d_normed = jnp.einsum("te,de->td", d_projected_b, full_qkv, preferred_element_type=jnp.float32)
    d_flat_b, d_gain_in = back_one(d_normed)
    grad_tokens = (d_flat_a + d_flat_b).reshape(tokens.shape)
    grad_gain_all = jnp.concatenate(
        [d_gain_in, d_gain_attn, d_gain_pre, d_gain_post, d_gain_query, d_gain_key]
    )
    if kernels:
        gain_terms = grad_gain_all.reshape(group_count, ctx_size, 1, gain_count)
        gain_terms = jnp.pad(gain_terms, ((0, 0), (0, 0), (0, 7), (0, 128 - gain_count)))
        gain_terms = gain_terms.transpose(1, 2, 0, 3).reshape(ctx_size * 8, group_count * 128)
        gain_sum, final_qkv = scatter(
            (gain_terms, grad_qkv.astype(jnp.bfloat16)), (False, True), None, 3, "scatter_qkv"
        )
        final_gains = gain_sum[0, :gain_count]
    else:
        final_qkv = scatter_all(grad_qkv)
        final_gains = lax.psum_scatter(
            grad_gain_all, ("batch", "ctx"), scatter_dimension=0, tiled=True
        )
    return (
        result,
        grad_tokens,
        final_qkv,
        final_out.T,
        final_gu,
        final_down.T,
        final_gains,
    )


def solution(mesh):
    in_specs = (
        P("batch", "ctx", None),
        P("ctx", "batch"),
        P("batch", "ctx"),
        P("ctx", "batch"),
        P("batch", "ctx"),
        P(("batch", "ctx")),
        P(),
        P("batch", "ctx", None),
    )
    out_specs = (
        P("batch", "ctx", None),
        P("batch", "ctx", None),
        P("ctx", "batch"),
        P("batch", "ctx"),
        P("ctx", "batch"),
        P("batch", "ctx"),
        P(("batch", "ctx")),
    )
    return jax.shard_map(body, mesh=mesh, in_specs=in_specs, out_specs=out_specs, check_vma=False)
```

```python
import jax
import jax.numpy as jnp
from jax import lax
from jax.experimental import pallas as pl
from jax.experimental.pallas import tpu as pltpu
from jax.sharding import PartitionSpec as P

D = 640
H = 4
HD = 256
FF = 2048


rope_base = 1000000.0
epsilon = 1e-06
neg_large = -1e30


def rms_scale(values, gain_vec):
    mean_square = jnp.mean(values * values, axis=-1, keepdims=True)
    return values * lax.rsqrt(mean_square + epsilon) * (1.0 + gain_vec)


def gelu_tanh(values):
    return (
        0.5
        * values
        * (1.0 + jnp.tanh(0.7978845608028654 * (values + 0.044715 * values * values * values)))
    )


def rope_tables(positions, head_size):
    half_size = head_size // 2
    exponent = jnp.arange(half_size, dtype=jnp.float32) * (2.0 / head_size)
    frequency = rope_base ** (-exponent)
    angles = positions.astype(jnp.float32)[:, None] * frequency[None, :]
    return (jnp.cos(angles), jnp.sin(angles))


def rotate(values, cosines, sine_vals):
    half_size = values.shape[-1] // 2
    first_half = values[..., :half_size]
    second_half = values[..., half_size:]
    return jnp.concatenate(
        [
            first_half * cosines - second_half * sine_vals,
            second_half * cosines + first_half * sine_vals,
        ],
        axis=-1,
    )


def add_branch(branch, base_rows, gain_vec):
    return base_rows + rms_scale(branch, gain_vec)


def activate(gate_up):
    return gelu_tanh(gate_up[:, :FF]) * gate_up[:, FF:]


MESH = pl.DeviceIdType.MESH


def flip(index, bit):
    half = (index // bit) % 2
    return index + bit - 2 * bit * half


def along_line(chip):
    return [chip, flip(chip, 1), 2 - chip // 2, 3 - 3 * (chip // 2)]


def only_if(condition, action):
    if condition is None:
        action()
    else:
        pl.when(condition)(action)


def greet(others):
    barrier = pltpu.get_barrier_semaphore()
    for other in others:
        pl.semaphore_signal(barrier, inc=1, device_id=other, device_id_type=MESH)
    pl.semaphore_wait(barrier, len(others))


def gather_kernel(chips, y_first, stacked, with_rows, *refs):
    count = len(y_first)
    shards, refs = refs[:count], refs[count:]
    if with_rows:
        row_shard, refs = refs[0], refs[1:]
    wholes, refs = refs[:count], refs[count:]
    if with_rows:
        row_whole, refs = refs[0], refs[1:]
    own_sem, send_sem, recv_sem = refs[:3]
    mine = lax.axis_index("batch")
    place = lax.axis_index("ctx")
    lane, chip = place % 2, place // 2
    mate = flip(place, 1)
    over_x, over_y = flip(mine, 1), flip(mine, 2)
    corner = flip(over_x, 2)
    line = [there * 2 + lane for there in along_line(chip)]
    inner = (chip == 1) | (chip == 2)
    across = (3 - chip) * 2 + lane
    relay = [across, across, line[1], line[1]]
    greet(
        [(mine, mate), (over_x, place), (over_y, place), (mine, line[1]), (mine, across)]
    )

    def window(which, row_owner, place_owner):
        whole = wholes[which]
        rows, width = shards[which].shape
        if stacked[which]:
            start = pl.multiple_of((row_owner * (2 * chips) + place_owner) * rows, rows)
            return whole.at[pl.ds(start, rows), :]
        return whole.at[
            pl.ds(pl.multiple_of(place_owner * rows, rows), rows),
            pl.ds(pl.multiple_of(row_owner * width, 128), width),
        ]

    sent = []
    used = [0] * count

    def send(which, row_owner, place_owner, target, source=None, condition=None):
        copy = pltpu.make_async_remote_copy(
            src_ref=window(which, row_owner, place_owner) if source is None else source,
            dst_ref=window(which, row_owner, place_owner),
            send_sem=send_sem.at[which, used[which]],
            recv_sem=recv_sem.at[which, row_owner, place_owner],
            device_id=target,
            device_id_type=MESH,
        )
        used[which] += 1
        only_if(condition, copy.start)
        sent.append((condition, copy))

    def arrived(which, row_owner, place_owner):
        pltpu.make_async_copy(
            window(which, row_owner, place_owner),
            window(which, row_owner, place_owner),
            recv_sem.at[which, row_owner, place_owner],
        ).wait()

    first = [over_y if y else over_x for y in y_first]
    second = [over_x if y else over_y for y in y_first]
    own = []
    for which in range(count):
        copy = pltpu.make_async_copy(
            shards[which], window(which, mine, place), own_sem.at[which]
        )
        copy.start()
        own.append(copy)
        source = shards[which]
        send(which, mine, place, (mine, line[1]), source)
        send(which, mine, place, (mine, across), source, inner)
        send(which, mine, place, (first[which], place), source)
        send(which, mine, place, (second[which], place), source)
        send(which, mine, place, (mine, mate), source)
    if with_rows:
        rows_own_sem, rows_send_sem, rows_recv_sem = refs[3:]
        row_count = row_shard.shape[1]

        def row_window(owner):
            start = pl.multiple_of(owner * row_count, row_count)
            return row_whole.at[:, pl.ds(start, row_count), :]

        def send_rows(slot, owner, target, source, condition=None):
            copy = pltpu.make_async_remote_copy(
                src_ref=source,
                dst_ref=row_window(owner),
                send_sem=rows_send_sem.at[slot],
                recv_sem=rows_recv_sem.at[owner],
                device_id=(mine, target),
                device_id_type=MESH,
            )
            only_if(condition, copy.start)
            sent.append((condition, copy))

        def rows_arrived(owner):
            pltpu.make_async_copy(
                row_window(owner), row_window(owner), rows_recv_sem.at[owner]
            ).wait()

        copy = pltpu.make_async_copy(row_shard, row_window(place), rows_own_sem)
        copy.start()
        own.append(copy)
        send_rows(0, place, line[1], row_shard)
        send_rows(1, place, across, row_shard, inner)
        send_rows(2, place, mate, row_shard)
    for step in range(chips):
        for which in range(count):
            if step > 0:
                arrived(which, mine, line[step])
                send(which, mine, line[step], (mine, relay[step]), None, inner)
                send(which, mine, line[step], (first[which], place))
                send(which, mine, line[step], (second[which], place))
                send(which, mine, line[step], (mine, mate))
        for which in range(count):
            arrived(which, first[which], line[step])
            send(which, first[which], line[step], (second[which], place))
            send(which, first[which], line[step], (mine, mate))
        if with_rows and step > 0:
            rows_arrived(line[step])
            send_rows(2 * step + 1, line[step], relay[step], row_window(line[step]), inner)
            send_rows(2 * step + 2, line[step], mate, row_window(line[step]))
    for step in range(chips):
        for which in range(count):
            arrived(which, second[which], line[step])
            send(which, second[which], line[step], (mine, mate))
        for which in range(count):
            arrived(which, corner, line[step])
            send(which, corner, line[step], (mine, mate))
    if with_rows:
        for step in range(chips):
            rows_arrived(flip(line[step], 1))
    for step in range(chips):
        for which in range(count):
            for row_owner in (mine, over_x, over_y, corner):
                arrived(which, row_owner, flip(line[step], 1))
    for copy in own:
        copy.wait()
    for condition, copy in sent:
        only_if(condition, copy.wait_send)


def gather(shards, y_first, stacked, rows, collective_id, name):
    groups, places = lax.axis_size("batch"), lax.axis_size("ctx")
    chips = places // 2
    count = len(shards)
    shapes = [
        (groups * places * piece.shape[0], piece.shape[1])
        if under
        else (places * piece.shape[0], groups * piece.shape[1])
        for piece, under in zip(shards, stacked)
    ]
    operands = list(shards)
    scratch = [
        pltpu.SemaphoreType.DMA((count,)),
        pltpu.SemaphoreType.DMA((count, 10 * chips)),
        pltpu.SemaphoreType.DMA((count, groups, places)),
    ]
    if rows is not None:
        operands.append(rows)
        shapes.append((rows.shape[0], places * rows.shape[1], rows.shape[2]))
        scratch += [
            pltpu.SemaphoreType.DMA(()),
            pltpu.SemaphoreType.DMA((3 * chips,)),
            pltpu.SemaphoreType.DMA((places,)),
        ]
    any_space = pl.BlockSpec(memory_space=pl.ANY)
    return pl.pallas_call(
        lambda *refs: gather_kernel(chips, y_first, stacked, rows is not None, *refs),
        out_shape=[jax.ShapeDtypeStruct(shape, jnp.bfloat16) for shape in shapes],
        in_specs=[any_space] * len(operands),
        out_specs=[any_space] * len(operands),
        scratch_shapes=scratch,
        compiler_params=pltpu.CompilerParams(collective_id=collective_id, has_side_effects=True),
        name=name,
    )(*operands)


def scatter_kernel(chips, y_first, with_rows, *refs):
    count = len(y_first)
    total = count + (1 if with_rows else 0)
    terms, refs = refs[:total], refs[total:]
    outs, refs = refs[:total], refs[total:]
    held, refs = refs[:total], refs[total:]
    got_mate, refs = refs[:total], refs[total:]
    got_first, refs = refs[:count], refs[count:]
    got_second, refs = refs[:count], refs[count:]
    got_line, refs = refs[:total], refs[total:]
    own_sem, mate_sem, first_sem, second_sem, line_send_sem, line_recv_sem = refs
    mine = lax.axis_index("batch")
    place = lax.axis_index("ctx")
    lane, chip = place % 2, place // 2
    mate = flip(place, 1)
    over_x, over_y = flip(mine, 1), flip(mine, 2)
    first = [over_y if y else over_x for y in y_first]
    second = [over_x if y else over_y for y in y_first]
    bit = [1 if y else 2 for y in y_first]
    chips_at = along_line(chip)
    beside = chips_at[1] * 2 + lane
    across = (3 - chip) * 2 + lane
    inner = (chip == 1) | (chip == 2)
    outer = (chip == 0) | (chip == 3)
    greet([(mine, mate), (over_x, place), (over_y, place), (mine, beside), (mine, across)])
    sent = []

    def send(source, target, sems, slot, device, condition=None):
        copy = pltpu.make_async_remote_copy(
            src_ref=source,
            dst_ref=target,
            send_sem=sems.at[(0, *slot)],
            recv_sem=sems.at[(1, *slot)],
            device_id=device,
            device_id_type=MESH,
        )
        only_if(condition, copy.start)
        sent.append((condition, copy))

    def arrived(target, sems, slot):
        pltpu.make_async_copy(target, target, sems.at[(1, *slot)]).wait()

    def part(which, owner):
        if which == count:
            rows = outs[which].shape[1]
            return terms[which].at[:, pl.ds(pl.multiple_of(owner * rows, rows), rows), :]
        rows = outs[which].shape[0]
        return terms[which].at[pl.ds(pl.multiple_of(owner * rows, rows), rows), :]

    def in_groups(which, step):
        if which == count:
            pl.loop(0, outs[which].shape[0])(lambda i: step((i,)))
            return
        rows = outs[which].shape[0]
        group = 16 if rows % 16 == 0 else rows
        pl.loop(0, rows // group)(
            lambda i: step((pl.ds(pl.multiple_of(i * group, group), group),))
        )

    def columns(which, owner):
        width = outs[which].shape[1]
        return pl.ds(pl.multiple_of(owner * width, 128), width)

    order = list(range(chips - 1, -1, -1))
    own = {}
    whiches = ([count] if with_rows else []) + list(range(count))
    for d in order:
        for which in whiches:
            there = chips_at[d]
            send(
                part(which, there * 2 + 1 - lane),
                got_mate[which].at[there],
                mate_sem,
                (which, there),
                (mine, mate),
            )
            copy = pltpu.make_async_copy(
                part(which, there * 2 + lane), held[which].at[d], own_sem.at[which, d]
            )
            copy.start()
            own[which, d] = copy

    f32 = jnp.float32

    def sums(which):
        return got_mate[which] if which == count else got_second[which]

    def send_line(which, d, slot, target, condition, sem_slot):
        copy = pltpu.make_async_remote_copy(
            src_ref=sums(which).at[chips_at[d]],
            dst_ref=got_line[which].at[slot],
            send_sem=line_send_sem.at[which, sem_slot],
            recv_sem=line_recv_sem.at[which, slot],
            device_id=(mine, target),
            device_id_type=MESH,
        )
        only_if(condition, copy.start)
        sent.append((condition, copy))

    def line_arrived(which, slot):
        target = got_line[which].at[slot]
        pltpu.make_async_copy(target, target, line_recv_sem.at[which, slot]).wait()

    def send_out(which, d):
        if d > 0:
            send_line(which, d, d - 1, beside, outer, d - 1)

    def add_line(which, d, slot):
        @pl.when(inner)
        def _():
            line_arrived(which, slot)

            def add(spot):
                at = (chips_at[d], *spot)
                sums(which)[at] = (
                    sums(which)[at].astype(f32) + got_line[which][(slot, *spot)].astype(f32)
                ).astype(sums(which).dtype)

            in_groups(which, add)

    def pass_across(which):
        for d, slot in ((3, 4), (2, 3)):
            add_line(which, d, d - 1)
            send_line(which, d, slot, across, inner, slot)

    def pass_back(which):
        add_line(which, 1, 4)
        send_line(which, 1, 0, beside, inner, 5)

    for d in order:
        there = chips_at[d]
        for which in whiches:
            arrived(got_mate[which].at[there], mate_sem, (which, there))
            own[which, d].wait()

            def add_mate(spot, which=which, there=there, d=d):
                at = (there, *spot)
                got_mate[which][at] = (
                    got_mate[which][at].astype(f32) + held[which][(d, *spot)].astype(f32)
                ).astype(got_mate[which].dtype)

            in_groups(which, add_mate)
            if which == count:
                send_out(which, d)
                continue
            for slot, owner in ((1, flip(first[which], bit[which])), (0, first[which])):
                send(
                    got_mate[which].at[there, :, columns(which, owner)],
                    got_first[which].at[there, slot],
                    first_sem,
                    (which, there, slot),
                    (first[which], place),
                )
    for d in order:
        there = chips_at[d]
        for which in range(count):
            for slot, owner in ((1, second[which]), (0, mine)):
                arrived(got_first[which].at[there, slot], first_sem, (which, there, slot))

                def add_first(spot, which=which, there=there, slot=slot, owner=owner):
                    at = (there, slot, *spot)
                    got_first[which][at] = (
                        got_first[which][at].astype(f32)
                        + got_mate[which][(there, *spot, columns(which, owner))].astype(f32)
                    ).astype(got_first[which].dtype)

                in_groups(which, add_first)
                if slot == 1:
                    send(
                        got_first[which].at[there, 1],
                        got_second[which].at[there],
                        second_sem,
                        (which, there),
                        (second[which], place),
                    )
    if with_rows:
        pass_across(count)
    for d in order:
        there = chips_at[d]
        for which in range(count):
            arrived(got_second[which].at[there], second_sem, (which, there))
            if d == 0:
                continue

            def add_second(spot, which=which, there=there):
                at = (there, *spot)
                got_second[which][at] = (
                    got_second[which][at].astype(f32)
                    + got_first[which][(there, 0, *spot)].astype(f32)
                ).astype(got_second[which].dtype)

            in_groups(which, add_second)
            send_out(which, d)
    if with_rows:
        pass_back(count)
    for which in range(count):
        pass_across(which)
    for which in range(count):
        pass_back(which)
    for which in whiches:
        line_arrived(which, 0)

        def finish(spot, which=which):
            value = sums(which)[(chip, *spot)].astype(f32)
            if which < count:
                value = value + got_first[which][(chip, 0, *spot)].astype(f32)
            outs[which][spot] = value + got_line[which][(0, *spot)].astype(f32)

        in_groups(which, finish)

        @pl.when(inner)
        def _(which=which):
            line_arrived(which, 3)

            def add_across(spot):
                outs[which][spot] = outs[which][spot] + got_line[which][(3, *spot)].astype(f32)

            in_groups(which, add_across)

    for condition, copy in sent:
        only_if(condition, copy.wait_send)


def scatter(terms, y_first, rows, collective_id, name):
    groups, places = lax.axis_size("batch"), lax.axis_size("ctx")
    chips = places // 2
    pieces = [(term.shape[0] // places, term.shape[1] // groups) for term in terms]
    kinds = [term.dtype for term in terms]
    operands = list(terms)
    outs = list(pieces)
    wide = [(chips, piece[0], groups * piece[1]) for piece in pieces]
    if rows is not None:
        piece = (rows.shape[0], rows.shape[1] // places, rows.shape[2])
        operands.append(rows)
        outs.append(piece)
        wide.append((chips, *piece))
        kinds.append(rows.dtype)
    count, total = len(terms), len(operands)
    scratch = [pltpu.VMEM(shape, kind) for shape, kind in zip(wide, kinds)] * 2
    scratch += [pltpu.VMEM((chips, 2, *piece), kind) for piece, kind in zip(pieces, kinds)]
    scratch += [pltpu.VMEM((chips, *piece), kind) for piece, kind in zip(pieces, kinds)]
    scratch += [pltpu.VMEM((5, *piece), kind) for piece, kind in zip(outs, kinds)]
    scratch += [
        pltpu.SemaphoreType.DMA((total, chips)),
        pltpu.SemaphoreType.DMA((2, total, chips)),
        pltpu.SemaphoreType.DMA((2, count, chips, 2)),
        pltpu.SemaphoreType.DMA((2, count, chips)),
        pltpu.SemaphoreType.DMA((total, 6)),
        pltpu.SemaphoreType.DMA((total, 5)),
    ]
    return pl.pallas_call(
        lambda *refs: scatter_kernel(chips, y_first, rows is not None, *refs),
        out_shape=[jax.ShapeDtypeStruct(shape, jnp.float32) for shape in outs],
        in_specs=[pl.BlockSpec(memory_space=pl.ANY)] * total,
        out_specs=[pl.BlockSpec(memory_space=pltpu.VMEM)] * total,
        scratch_shapes=scratch,
        compiler_params=pltpu.CompilerParams(
            collective_id=collective_id, has_side_effects=True, vmem_limit_bytes=40 * 2**20
        ),
        name=name,
    )(*operands)


def fits_kernels(w_qkv):
    groups, places = lax.axis_size("batch"), lax.axis_size("ctx")
    return groups == 4 and places == 8 and w_qkv.shape[0] % 16 == 0


def gather_all(value, ctx_dim):
    part = lax.all_gather(value, "ctx", axis=ctx_dim, tiled=True)
    return lax.all_gather(part, "batch", axis=1 - ctx_dim, tiled=True)


def scatter_all(value):
    part = lax.psum_scatter(
        value.astype(jnp.bfloat16), "batch", scatter_dimension=1, tiled=True
    )
    return lax.psum_scatter(part, "ctx", scatter_dimension=0, tiled=True).astype(jnp.float32)


def body(tokens, w_qkv, w_out, w_gate_up, w_down, norm_gains, block_order, cotangent):
    seq_count, tok_rows, _ = tokens.shape
    block_len = tok_rows // 2
    ctx_index = lax.axis_index("ctx")
    score_scale = HD ** (-0.5)
    kernels = fits_kernels(w_qkv)
    group_count, ctx_size = lax.axis_size("batch"), lax.axis_size("ctx")
    device_count = group_count * ctx_size
    gain_count = norm_gains.shape[0]
    if kernels:
        gain_tile = jnp.pad(norm_gains[None, :], ((0, 15), (0, 128 - gain_count)))
        gain_tiles, full_qkv = gather(
            (gain_tile, w_qkv), (True, False), (True, False), None, 0, "gather_qkv"
        )
        full_gains = gain_tiles.reshape(device_count, 16, 128)[:, 0, :gain_count].reshape(-1)
    else:
        full_qkv = gather_all(w_qkv, 0)
        full_gains = lax.all_gather(norm_gains, ("batch", "ctx"), axis=0, tiled=True)
    gain_all = full_gains.astype(jnp.float32)
    gain_in = gain_all[0:D]
    gain_attn = gain_all[D : 2 * D]
    gain_pre = gain_all[2 * D : 3 * D]
    gain_post = gain_all[3 * D : 4 * D]
    gain_query = gain_all[4 * D : 4 * D + HD]
    gain_key = gain_all[4 * D + HD : 4 * D + 2 * HD]
    offsets = jnp.arange(block_len, dtype=jnp.int32)
    key_pos = (block_order[:, None] * block_len + offsets[None, :]).reshape(-1)
    query_pos = lax.dynamic_slice_in_dim(key_pos, ctx_index * tok_rows, tok_rows)
    cosines, sine_vals = rope_tables(query_pos, HD)
    flat = tokens.reshape(seq_count * tok_rows, D).astype(jnp.float32)
    normed, back_one = jax.vjp(rms_scale, flat, gain_in)
    normed_b = normed.astype(jnp.bfloat16)
    projected = jnp.dot(normed_b, full_qkv, preferred_element_type=jnp.float32)

    def prepare(raw_proj, gain_q, gain_k):
        shaped = raw_proj.reshape(seq_count, tok_rows, H + 2, HD)
        queries = rotate(
            rms_scale(shaped[:, :, :H], gain_q),
            cosines[None, :, None, :],
            sine_vals[None, :, None, :],
        )
        key_vecs = rotate(rms_scale(shaped[:, :, H], gain_k), cosines[None], sine_vals[None])
        return (queries.transpose(0, 2, 1, 3), key_vecs, shaped[:, :, H + 1])

    (queries, key_vecs, val_vecs), back_prep = jax.vjp(prepare, projected, gain_query, gain_key)
    query_b = queries.astype(jnp.bfloat16)
    key_b = key_vecs.astype(jnp.bfloat16)
    value_b = val_vecs.astype(jnp.bfloat16)

    key_value_own = jnp.concatenate([key_b, value_b], axis=-1)
    if kernels:
        full_out, full_down, full_gu, key_value = gather(
            (w_out.T, w_down.T, w_gate_up),
            (False, False, True),
            (False, False, False),
            key_value_own,
            1,
            "gather_rest",
        )
    else:
        full_out = gather_all(w_out, 1).T
        full_down = gather_all(w_down, 1).T
        full_gu = gather_all(w_gate_up, 0)
        key_value = lax.all_gather(key_value_own, "ctx", axis=1, tiled=True)
    key_piece, value_piece = key_value[..., :HD], key_value[..., HD:]
    allowed = key_pos[None, :] <= query_pos[:, None]
    raw_scores = (
        jnp.einsum("shrd,snd->shrn", query_b, key_piece, preferred_element_type=jnp.float32)
        * score_scale
    )
    scores = jnp.where(allowed, raw_scores, neg_large)
    row_max = jnp.max(scores, axis=-1, keepdims=True)
    powers = jnp.exp(scores - row_max)
    soft_b = (powers / jnp.sum(powers, axis=-1, keepdims=True)).astype(jnp.bfloat16)
    attn_out = jnp.einsum(
        "shrn,snd->shrd", soft_b, value_piece, preferred_element_type=jnp.float32
    )
    attn_b = (
        attn_out.transpose(0, 2, 1, 3).reshape(seq_count * tok_rows, H * HD).astype(jnp.bfloat16)
    )
    y_attn = jnp.einsum("te,de->td", attn_b, full_out, preferred_element_type=jnp.float32)
    residual, back_attn = jax.vjp(add_branch, y_attn, flat, gain_attn)
    normed_two, back_two = jax.vjp(rms_scale, residual, gain_pre)
    normed_two_b = normed_two.astype(jnp.bfloat16)
    gate_up = jnp.dot(normed_two_b, full_gu, preferred_element_type=jnp.float32)
    hidden, back_act = jax.vjp(activate, gate_up)
    hidden_b = hidden.astype(jnp.bfloat16)
    branch = jnp.einsum("tf,df->td", hidden_b, full_down, preferred_element_type=jnp.float32)
    output, back_out = jax.vjp(add_branch, branch, residual, gain_post)
    result = output.astype(jnp.bfloat16).reshape(tokens.shape)
    seed_grad = cotangent.reshape(seq_count * tok_rows, D).astype(jnp.float32)
    d_branch, d_resid_a, d_gain_post = back_out(seed_grad)
    d_branch_b = d_branch.astype(jnp.bfloat16)
    grad_down = jnp.einsum("td,tf->df", d_branch_b, hidden_b, preferred_element_type=jnp.float32)
    d_hidden = jnp.einsum("td,df->tf", d_branch_b, full_down, preferred_element_type=jnp.float32)
    (d_gate_up,) = back_act(d_hidden)
    d_gate_up_b = d_gate_up.astype(jnp.bfloat16)
    grad_gu = jnp.einsum("td,tf->df", normed_two_b, d_gate_up_b, preferred_element_type=jnp.float32)
    d_normed_two = jnp.einsum("tf,df->td", d_gate_up_b, full_gu, preferred_element_type=jnp.float32)
    d_resid_b, d_gain_pre = back_two(d_normed_two)
    d_y_attn, d_flat_a, d_gain_attn = back_attn(d_resid_a + d_resid_b)
    d_y_attn_b = d_y_attn.astype(jnp.bfloat16)
    grad_out = jnp.einsum("td,te->de", d_y_attn_b, attn_b, preferred_element_type=jnp.float32)
    d_attn_rows = jnp.einsum(
        "td,de->te", d_y_attn_b, full_out, preferred_element_type=jnp.float32
    ).astype(jnp.bfloat16)
    d_attn = d_attn_rows.reshape(seq_count, tok_rows, H, HD).transpose(0, 2, 1, 3)
    row_dot = jnp.sum(d_attn.astype(jnp.float32) * attn_out, axis=-1)

    d_probs = jnp.einsum(
        "shrd,snd->shrn", d_attn, value_piece, preferred_element_type=jnp.float32
    )
    d_scores = (soft_b.astype(jnp.float32) * (d_probs - row_dot[..., None])).astype(jnp.bfloat16)
    d_key = (
        jnp.einsum("shrn,shrd->snd", d_scores, query_b, preferred_element_type=jnp.float32)
        * score_scale
    )
    d_value = jnp.einsum("shrn,shrd->snd", soft_b, d_attn, preferred_element_type=jnp.float32)
    d_key_value_all = jnp.concatenate([d_key, d_value], axis=-1).astype(jnp.bfloat16)
    if kernels:
        final_out, final_down, final_gu, d_key_value = scatter(
            (
                grad_out.astype(jnp.bfloat16),
                grad_down.astype(jnp.bfloat16),
                grad_gu.astype(jnp.bfloat16),
            ),
            (True, True, False),
            d_key_value_all,
            2,
            "scatter_rest",
        )
    else:
        final_out, final_down, final_gu = (
            scatter_all(grad_out),
            scatter_all(grad_down),
            scatter_all(grad_gu),
        )
        d_key_value = lax.psum_scatter(
            d_key_value_all, "ctx", scatter_dimension=1, tiled=True
        ).astype(jnp.float32)
    grad_key, grad_value = d_key_value[..., :HD], d_key_value[..., HD:]
    grad_query = (
        jnp.einsum("shrn,snd->shrd", d_scores, key_piece, preferred_element_type=jnp.float32)
        * score_scale
    )
    d_projected, d_gain_query, d_gain_key = back_prep((grad_query, grad_key, grad_value))
    d_projected_b = d_projected.astype(jnp.bfloat16)
    grad_qkv = jnp.einsum("td,te->de", normed_b, d_projected_b, preferred_element_type=jnp.float32)
    d_normed = jnp.einsum("te,de->td", d_projected_b, full_qkv, preferred_element_type=jnp.float32)
    d_flat_b, d_gain_in = back_one(d_normed)
    grad_tokens = (d_flat_a + d_flat_b).reshape(tokens.shape)
    grad_gain_all = jnp.concatenate(
        [d_gain_in, d_gain_attn, d_gain_pre, d_gain_post, d_gain_query, d_gain_key]
    )
    if kernels:
        gain_terms = grad_gain_all.reshape(group_count, ctx_size, 1, gain_count)
        gain_terms = jnp.pad(gain_terms, ((0, 0), (0, 0), (0, 7), (0, 128 - gain_count)))
        gain_terms = gain_terms.transpose(1, 2, 0, 3).reshape(ctx_size * 8, group_count * 128)
        gain_sum, final_qkv = scatter(
            (gain_terms, grad_qkv.astype(jnp.bfloat16)), (False, True), None, 3, "scatter_qkv"
        )
        final_gains = gain_sum[0, :gain_count]
    else:
        final_qkv = scatter_all(grad_qkv)
        final_gains = lax.psum_scatter(
            grad_gain_all, ("batch", "ctx"), scatter_dimension=0, tiled=True
        )
    return (
        result,
        grad_tokens,
        final_qkv,
        final_out.T,
        final_gu,
        final_down.T,
        final_gains,
    )


def solution(mesh):
    in_specs = (
        P("batch", "ctx", None),
        P("ctx", "batch"),
        P("batch", "ctx"),
        P("ctx", "batch"),
        P("batch", "ctx"),
        P(("batch", "ctx")),
        P(),
        P("batch", "ctx", None),
    )
    out_specs = (
        P("batch", "ctx", None),
        P("batch", "ctx", None),
        P("ctx", "batch"),
        P("batch", "ctx"),
        P("ctx", "batch"),
        P("batch", "ctx"),
        P(("batch", "ctx")),
    )
    return jax.shard_map(body, mesh=mesh, in_specs=in_specs, out_specs=out_specs, check_vma=False)
```

```python
import jax
import jax.numpy as jnp
from jax import lax
from jax.experimental import pallas as pl
from jax.experimental.pallas import tpu as pltpu
from jax.sharding import PartitionSpec as P

D = 640
H = 4
HD = 256
FF = 2048


rope_base = 1000000.0
epsilon = 1e-06
neg_large = -1e30


def rms_scale(values, gain_vec):
    mean_square = jnp.mean(values * values, axis=-1, keepdims=True)
    return values * lax.rsqrt(mean_square + epsilon) * (1.0 + gain_vec)


def gelu_tanh(values):
    return (
        0.5
        * values
        * (1.0 + jnp.tanh(0.7978845608028654 * (values + 0.044715 * values * values * values)))
    )


def rope_tables(positions, head_size):
    half_size = head_size // 2
    exponent = jnp.arange(half_size, dtype=jnp.float32) * (2.0 / head_size)
    frequency = rope_base ** (-exponent)
    angles = positions.astype(jnp.float32)[:, None] * frequency[None, :]
    return (jnp.cos(angles), jnp.sin(angles))


def rotate(values, cosines, sine_vals):
    half_size = values.shape[-1] // 2
    first_half = values[..., :half_size]
    second_half = values[..., half_size:]
    return jnp.concatenate(
        [
            first_half * cosines - second_half * sine_vals,
            second_half * cosines + first_half * sine_vals,
        ],
        axis=-1,
    )


def add_branch(branch, base_rows, gain_vec):
    return base_rows + rms_scale(branch, gain_vec)


def activate(gate_up):
    return gelu_tanh(gate_up[:, :FF]) * gate_up[:, FF:]


MESH = pl.DeviceIdType.MESH


def flip(index, bit):
    half = (index // bit) % 2
    return index + bit - 2 * bit * half


def along_line(chip):
    return [chip, flip(chip, 1), 2 - chip // 2, 3 - 3 * (chip // 2)]


def only_if(condition, action):
    if condition is None:
        action()
    else:
        pl.when(condition)(action)


def greet(others):
    barrier = pltpu.get_barrier_semaphore()
    for other in others:
        pl.semaphore_signal(barrier, inc=1, device_id=other, device_id_type=MESH)
    pl.semaphore_wait(barrier, len(others))


def gather_kernel(chips, y_first, stacked, with_rows, *refs):
    count = len(y_first)
    shards, refs = refs[:count], refs[count:]
    if with_rows:
        row_shard, refs = refs[0], refs[1:]
    wholes, refs = refs[:count], refs[count:]
    if with_rows:
        row_whole, refs = refs[0], refs[1:]
    own_sem, send_sem, recv_sem = refs[:3]
    mine = lax.axis_index("batch")
    place = lax.axis_index("ctx")
    lane, chip = place % 2, place // 2
    mate = flip(place, 1)
    over_x, over_y = flip(mine, 1), flip(mine, 2)
    corner = flip(over_x, 2)
    line = [there * 2 + lane for there in along_line(chip)]
    inner = (chip == 1) | (chip == 2)
    across = (3 - chip) * 2 + lane
    relay = [across, across, line[1], line[1]]
    greet(
        [(mine, mate), (over_x, place), (over_y, place), (mine, line[1]), (mine, across)]
    )

    def window(which, row_owner, place_owner):
        whole = wholes[which]
        rows, width = shards[which].shape
        if stacked[which]:
            start = pl.multiple_of((row_owner * (2 * chips) + place_owner) * rows, rows)
            return whole.at[pl.ds(start, rows), :]
        return whole.at[
            pl.ds(pl.multiple_of(place_owner * rows, rows), rows),
            pl.ds(pl.multiple_of(row_owner * width, 128), width),
        ]

    sent = []
    used = [0] * count

    def send(which, row_owner, place_owner, target, source=None, condition=None):
        copy = pltpu.make_async_remote_copy(
            src_ref=window(which, row_owner, place_owner) if source is None else source,
            dst_ref=window(which, row_owner, place_owner),
            send_sem=send_sem.at[which, used[which]],
            recv_sem=recv_sem.at[which, row_owner, place_owner],
            device_id=target,
            device_id_type=MESH,
        )
        used[which] += 1
        only_if(condition, copy.start)
        sent.append((condition, copy))

    def arrived(which, row_owner, place_owner):
        pltpu.make_async_copy(
            window(which, row_owner, place_owner),
            window(which, row_owner, place_owner),
            recv_sem.at[which, row_owner, place_owner],
        ).wait()

    first = [over_y if y else over_x for y in y_first]
    second = [over_x if y else over_y for y in y_first]
    own = []
    for which in range(count):
        copy = pltpu.make_async_copy(
            shards[which], window(which, mine, place), own_sem.at[which]
        )
        copy.start()
        own.append(copy)
        source = shards[which]
        send(which, mine, place, (mine, line[1]), source)
        send(which, mine, place, (mine, across), source, inner)
        send(which, mine, place, (first[which], place), source)
        send(which, mine, place, (second[which], place), source)
        send(which, mine, place, (mine, mate), source)
    if with_rows:
        rows_own_sem, rows_send_sem, rows_recv_sem = refs[3:]
        row_count = row_shard.shape[1]

        def row_window(owner):
            start = pl.multiple_of(owner * row_count, row_count)
            return row_whole.at[:, pl.ds(start, row_count), :]

        def send_rows(slot, owner, target, source, condition=None):
            copy = pltpu.make_async_remote_copy(
                src_ref=source,
                dst_ref=row_window(owner),
                send_sem=rows_send_sem.at[slot],
                recv_sem=rows_recv_sem.at[owner],
                device_id=(mine, target),
                device_id_type=MESH,
            )
            only_if(condition, copy.start)
            sent.append((condition, copy))

        def rows_arrived(owner):
            pltpu.make_async_copy(
                row_window(owner), row_window(owner), rows_recv_sem.at[owner]
            ).wait()

        copy = pltpu.make_async_copy(row_shard, row_window(place), rows_own_sem)
        copy.start()
        own.append(copy)

        def pass_rows(step):
            rows_arrived(line[step])
            send_rows(2 * step + 1, line[step], relay[step], row_window(line[step]), inner)
            send_rows(2 * step + 2, line[step], mate, row_window(line[step]))

    for step in range(chips):
        for which in range(count):
            if step > 0:
                arrived(which, mine, line[step])
                send(which, mine, line[step], (mine, relay[step]), None, inner)
                send(which, mine, line[step], (first[which], place))
                send(which, mine, line[step], (second[which], place))
                send(which, mine, line[step], (mine, mate))
        for which in range(count):
            arrived(which, first[which], line[step])
            send(which, first[which], line[step], (second[which], place))
            send(which, first[which], line[step], (mine, mate))
        if with_rows and step == 1:
            send_rows(0, place, line[1], row_shard)
            send_rows(1, place, across, row_shard, inner)
            send_rows(2, place, mate, row_shard)
    if with_rows:
        pass_rows(1)
    for step in range(chips):
        for which in range(count):
            arrived(which, second[which], line[step])
            send(which, second[which], line[step], (mine, mate))
        for which in range(count):
            arrived(which, corner, line[step])
            send(which, corner, line[step], (mine, mate))
        if with_rows and step in (0, 2):
            pass_rows(2 + step // 2)
    if with_rows:
        for step in range(chips):
            rows_arrived(flip(line[step], 1))
    for step in range(chips):
        for which in range(count):
            for row_owner in (mine, over_x, over_y, corner):
                arrived(which, row_owner, flip(line[step], 1))
    for copy in own:
        copy.wait()
    for condition, copy in sent:
        only_if(condition, copy.wait_send)


def gather(shards, y_first, stacked, rows, collective_id, name):
    groups, places = lax.axis_size("batch"), lax.axis_size("ctx")
    chips = places // 2
    count = len(shards)
    shapes = [
        (groups * places * piece.shape[0], piece.shape[1])
        if under
        else (places * piece.shape[0], groups * piece.shape[1])
        for piece, under in zip(shards, stacked)
    ]
    operands = list(shards)
    scratch = [
        pltpu.SemaphoreType.DMA((count,)),
        pltpu.SemaphoreType.DMA((count, 10 * chips)),
        pltpu.SemaphoreType.DMA((count, groups, places)),
    ]
    if rows is not None:
        operands.append(rows)
        shapes.append((rows.shape[0], places * rows.shape[1], rows.shape[2]))
        scratch += [
            pltpu.SemaphoreType.DMA(()),
            pltpu.SemaphoreType.DMA((3 * chips,)),
            pltpu.SemaphoreType.DMA((places,)),
        ]
    any_space = pl.BlockSpec(memory_space=pl.ANY)
    return pl.pallas_call(
        lambda *refs: gather_kernel(chips, y_first, stacked, rows is not None, *refs),
        out_shape=[jax.ShapeDtypeStruct(shape, jnp.bfloat16) for shape in shapes],
        in_specs=[any_space] * len(operands),
        out_specs=[any_space] * len(operands),
        scratch_shapes=scratch,
        compiler_params=pltpu.CompilerParams(collective_id=collective_id, has_side_effects=True),
        name=name,
    )(*operands)


def scatter_kernel(chips, y_first, with_rows, *refs):
    count = len(y_first)
    total = count + (1 if with_rows else 0)
    terms, refs = refs[:total], refs[total:]
    outs, refs = refs[:total], refs[total:]
    held, refs = refs[:total], refs[total:]
    got_mate, refs = refs[:total], refs[total:]
    got_first, refs = refs[:count], refs[count:]
    got_second, refs = refs[:count], refs[count:]
    got_line, refs = refs[:total], refs[total:]
    own_sem, mate_sem, first_sem, second_sem, line_send_sem, line_recv_sem = refs
    mine = lax.axis_index("batch")
    place = lax.axis_index("ctx")
    lane, chip = place % 2, place // 2
    mate = flip(place, 1)
    over_x, over_y = flip(mine, 1), flip(mine, 2)
    first = [over_y if y else over_x for y in y_first]
    second = [over_x if y else over_y for y in y_first]
    bit = [1 if y else 2 for y in y_first]
    chips_at = along_line(chip)
    beside = chips_at[1] * 2 + lane
    across = (3 - chip) * 2 + lane
    inner = (chip == 1) | (chip == 2)
    outer = (chip == 0) | (chip == 3)
    greet([(mine, mate), (over_x, place), (over_y, place), (mine, beside), (mine, across)])
    sent = []

    def send(source, target, sems, slot, device, condition=None):
        copy = pltpu.make_async_remote_copy(
            src_ref=source,
            dst_ref=target,
            send_sem=sems.at[(0, *slot)],
            recv_sem=sems.at[(1, *slot)],
            device_id=device,
            device_id_type=MESH,
        )
        only_if(condition, copy.start)
        sent.append((condition, copy))

    def arrived(target, sems, slot):
        pltpu.make_async_copy(target, target, sems.at[(1, *slot)]).wait()

    def part(which, owner):
        if which == count:
            rows = outs[which].shape[1]
            return terms[which].at[:, pl.ds(pl.multiple_of(owner * rows, rows), rows), :]
        rows = outs[which].shape[0]
        return terms[which].at[pl.ds(pl.multiple_of(owner * rows, rows), rows), :]

    def in_groups(which, step):
        if which == count:
            pl.loop(0, outs[which].shape[0])(lambda i: step((i,)))
            return
        rows = outs[which].shape[0]
        group = 16 if rows % 16 == 0 else rows
        pl.loop(0, rows // group)(
            lambda i: step((pl.ds(pl.multiple_of(i * group, group), group),))
        )

    def columns(which, owner):
        width = outs[which].shape[1]
        return pl.ds(pl.multiple_of(owner * width, 128), width)

    order = list(range(chips - 1, -1, -1))
    own = {}
    whiches = ([count] if with_rows else []) + list(range(count))
    for d in order:
        for which in whiches:
            there = chips_at[d]
            send(
                part(which, there * 2 + 1 - lane),
                got_mate[which].at[there],
                mate_sem,
                (which, there),
                (mine, mate),
            )
            copy = pltpu.make_async_copy(
                part(which, there * 2 + lane), held[which].at[d], own_sem.at[which, d]
            )
            copy.start()
            own[which, d] = copy

    f32 = jnp.float32

    def sums(which):
        return got_mate[which] if which == count else got_second[which]

    def send_line(which, d, slot, target, condition, sem_slot):
        copy = pltpu.make_async_remote_copy(
            src_ref=sums(which).at[chips_at[d]],
            dst_ref=got_line[which].at[slot],
            send_sem=line_send_sem.at[which, sem_slot],
            recv_sem=line_recv_sem.at[which, slot],
            device_id=(mine, target),
            device_id_type=MESH,
        )
        only_if(condition, copy.start)
        sent.append((condition, copy))

    def line_arrived(which, slot):
        target = got_line[which].at[slot]
        pltpu.make_async_copy(target, target, line_recv_sem.at[which, slot]).wait()

    def send_out(which, d):
        if d > 0:
            send_line(which, d, d - 1, beside, outer, d - 1)

    def add_line(which, d, slot):
        @pl.when(inner)
        def _():
            line_arrived(which, slot)

            def add(spot):
                at = (chips_at[d], *spot)
                sums(which)[at] = (
                    sums(which)[at].astype(f32) + got_line[which][(slot, *spot)].astype(f32)
                ).astype(sums(which).dtype)

            in_groups(which, add)

    def pass_across(which):
        for d, slot in ((3, 4), (2, 3)):
            add_line(which, d, d - 1)
            send_line(which, d, slot, across, inner, slot)

    def pass_back(which):
        add_line(which, 1, 4)
        send_line(which, 1, 0, beside, inner, 5)

    for d in order:
        there = chips_at[d]
        for which in whiches:
            arrived(got_mate[which].at[there], mate_sem, (which, there))
            own[which, d].wait()

            def add_mate(spot, which=which, there=there, d=d):
                at = (there, *spot)
                got_mate[which][at] = (
                    got_mate[which][at].astype(f32) + held[which][(d, *spot)].astype(f32)
                ).astype(got_mate[which].dtype)

            in_groups(which, add_mate)
            if which == count:
                send_out(which, d)
                continue
            for slot, owner in ((1, flip(first[which], bit[which])), (0, first[which])):
                send(
                    got_mate[which].at[there, :, columns(which, owner)],
                    got_first[which].at[there, slot],
                    first_sem,
                    (which, there, slot),
                    (first[which], place),
                )
    for d in order:
        there = chips_at[d]
        for which in range(count):
            for slot, owner in ((1, second[which]), (0, mine)):
                arrived(got_first[which].at[there, slot], first_sem, (which, there, slot))

                def add_first(spot, which=which, there=there, slot=slot, owner=owner):
                    at = (there, slot, *spot)
                    got_first[which][at] = (
                        got_first[which][at].astype(f32)
                        + got_mate[which][(there, *spot, columns(which, owner))].astype(f32)
                    ).astype(got_first[which].dtype)

                in_groups(which, add_first)
                if slot == 1:
                    send(
                        got_first[which].at[there, 1],
                        got_second[which].at[there],
                        second_sem,
                        (which, there),
                        (second[which], place),
                    )
    if with_rows:
        pass_across(count)
    for d in order:
        there = chips_at[d]
        for which in range(count):
            arrived(got_second[which].at[there], second_sem, (which, there))
            if d == 0:
                continue

            def add_second(spot, which=which, there=there):
                at = (there, *spot)
                got_second[which][at] = (
                    got_second[which][at].astype(f32)
                    + got_first[which][(there, 0, *spot)].astype(f32)
                ).astype(got_second[which].dtype)

            in_groups(which, add_second)
            send_out(which, d)
    if with_rows:
        pass_back(count)
    for which in range(count):
        pass_across(which)
    for which in range(count):
        pass_back(which)
    for which in whiches:
        line_arrived(which, 0)

        def finish(spot, which=which):
            value = sums(which)[(chip, *spot)].astype(f32)
            if which < count:
                value = value + got_first[which][(chip, 0, *spot)].astype(f32)
            outs[which][spot] = value + got_line[which][(0, *spot)].astype(f32)

        in_groups(which, finish)

        @pl.when(inner)
        def _(which=which):
            line_arrived(which, 3)

            def add_across(spot):
                outs[which][spot] = outs[which][spot] + got_line[which][(3, *spot)].astype(f32)

            in_groups(which, add_across)

    for condition, copy in sent:
        only_if(condition, copy.wait_send)


def scatter(terms, y_first, rows, collective_id, name):
    groups, places = lax.axis_size("batch"), lax.axis_size("ctx")
    chips = places // 2
    pieces = [(term.shape[0] // places, term.shape[1] // groups) for term in terms]
    kinds = [term.dtype for term in terms]
    operands = list(terms)
    outs = list(pieces)
    wide = [(chips, piece[0], groups * piece[1]) for piece in pieces]
    if rows is not None:
        piece = (rows.shape[0], rows.shape[1] // places, rows.shape[2])
        operands.append(rows)
        outs.append(piece)
        wide.append((chips, *piece))
        kinds.append(rows.dtype)
    count, total = len(terms), len(operands)
    scratch = [pltpu.VMEM(shape, kind) for shape, kind in zip(wide, kinds)] * 2
    scratch += [pltpu.VMEM((chips, 2, *piece), kind) for piece, kind in zip(pieces, kinds)]
    scratch += [pltpu.VMEM((chips, *piece), kind) for piece, kind in zip(pieces, kinds)]
    scratch += [pltpu.VMEM((5, *piece), kind) for piece, kind in zip(outs, kinds)]
    scratch += [
        pltpu.SemaphoreType.DMA((total, chips)),
        pltpu.SemaphoreType.DMA((2, total, chips)),
        pltpu.SemaphoreType.DMA((2, count, chips, 2)),
        pltpu.SemaphoreType.DMA((2, count, chips)),
        pltpu.SemaphoreType.DMA((total, 6)),
        pltpu.SemaphoreType.DMA((total, 5)),
    ]
    return pl.pallas_call(
        lambda *refs: scatter_kernel(chips, y_first, rows is not None, *refs),
        out_shape=[jax.ShapeDtypeStruct(shape, jnp.float32) for shape in outs],
        in_specs=[pl.BlockSpec(memory_space=pl.ANY)] * total,
        out_specs=[pl.BlockSpec(memory_space=pltpu.VMEM)] * total,
        scratch_shapes=scratch,
        compiler_params=pltpu.CompilerParams(
            collective_id=collective_id, has_side_effects=True, vmem_limit_bytes=40 * 2**20
        ),
        name=name,
    )(*operands)


def fits_kernels(w_qkv):
    groups, places = lax.axis_size("batch"), lax.axis_size("ctx")
    return groups == 4 and places == 8 and w_qkv.shape[0] % 16 == 0


def gather_all(value, ctx_dim):
    part = lax.all_gather(value, "ctx", axis=ctx_dim, tiled=True)
    return lax.all_gather(part, "batch", axis=1 - ctx_dim, tiled=True)


def scatter_all(value):
    part = lax.psum_scatter(
        value.astype(jnp.bfloat16), "batch", scatter_dimension=1, tiled=True
    )
    return lax.psum_scatter(part, "ctx", scatter_dimension=0, tiled=True).astype(jnp.float32)


def body(tokens, w_qkv, w_out, w_gate_up, w_down, norm_gains, block_order, cotangent):
    seq_count, tok_rows, _ = tokens.shape
    block_len = tok_rows // 2
    ctx_index = lax.axis_index("ctx")
    score_scale = HD ** (-0.5)
    kernels = fits_kernels(w_qkv)
    group_count, ctx_size = lax.axis_size("batch"), lax.axis_size("ctx")
    device_count = group_count * ctx_size
    gain_count = norm_gains.shape[0]
    if kernels:
        gain_tile = jnp.pad(norm_gains[None, :], ((0, 15), (0, 128 - gain_count)))
        gain_tiles, full_qkv = gather(
            (gain_tile, w_qkv), (True, False), (True, False), None, 0, "gather_qkv"
        )
        full_gains = gain_tiles.reshape(device_count, 16, 128)[:, 0, :gain_count].reshape(-1)
    else:
        full_qkv = gather_all(w_qkv, 0)
        full_gains = lax.all_gather(norm_gains, ("batch", "ctx"), axis=0, tiled=True)
    gain_all = full_gains.astype(jnp.float32)
    gain_in = gain_all[0:D]
    gain_attn = gain_all[D : 2 * D]
    gain_pre = gain_all[2 * D : 3 * D]
    gain_post = gain_all[3 * D : 4 * D]
    gain_query = gain_all[4 * D : 4 * D + HD]
    gain_key = gain_all[4 * D + HD : 4 * D + 2 * HD]
    offsets = jnp.arange(block_len, dtype=jnp.int32)
    key_pos = (block_order[:, None] * block_len + offsets[None, :]).reshape(-1)
    query_pos = lax.dynamic_slice_in_dim(key_pos, ctx_index * tok_rows, tok_rows)
    cosines, sine_vals = rope_tables(query_pos, HD)
    flat = tokens.reshape(seq_count * tok_rows, D).astype(jnp.float32)
    normed, back_one = jax.vjp(rms_scale, flat, gain_in)
    normed_b = normed.astype(jnp.bfloat16)
    projected = jnp.dot(normed_b, full_qkv, preferred_element_type=jnp.float32)

    def prepare(raw_proj, gain_q, gain_k):
        shaped = raw_proj.reshape(seq_count, tok_rows, H + 2, HD)
        queries = rotate(
            rms_scale(shaped[:, :, :H], gain_q),
            cosines[None, :, None, :],
            sine_vals[None, :, None, :],
        )
        key_vecs = rotate(rms_scale(shaped[:, :, H], gain_k), cosines[None], sine_vals[None])
        return (queries.transpose(0, 2, 1, 3), key_vecs, shaped[:, :, H + 1])

    (queries, key_vecs, val_vecs), back_prep = jax.vjp(prepare, projected, gain_query, gain_key)
    query_b = queries.astype(jnp.bfloat16)
    key_b = key_vecs.astype(jnp.bfloat16)
    value_b = val_vecs.astype(jnp.bfloat16)

    key_value_own = jnp.concatenate([key_b, value_b], axis=-1)
    if kernels:
        full_out, full_down, full_gu, key_value = gather(
            (w_out.T, w_down.T, w_gate_up),
            (False, False, True),
            (False, False, False),
            key_value_own,
            1,
            "gather_rest",
        )
    else:
        full_out = gather_all(w_out, 1).T
        full_down = gather_all(w_down, 1).T
        full_gu = gather_all(w_gate_up, 0)
        key_value = lax.all_gather(key_value_own, "ctx", axis=1, tiled=True)
    key_piece, value_piece = key_value[..., :HD], key_value[..., HD:]
    allowed = key_pos[None, :] <= query_pos[:, None]
    raw_scores = (
        jnp.einsum("shrd,snd->shrn", query_b, key_piece, preferred_element_type=jnp.float32)
        * score_scale
    )
    scores = jnp.where(allowed, raw_scores, neg_large)
    row_max = jnp.max(scores, axis=-1, keepdims=True)
    powers = jnp.exp(scores - row_max)
    soft_b = (powers / jnp.sum(powers, axis=-1, keepdims=True)).astype(jnp.bfloat16)
    attn_out = jnp.einsum(
        "shrn,snd->shrd", soft_b, value_piece, preferred_element_type=jnp.float32
    )
    attn_b = (
        attn_out.transpose(0, 2, 1, 3).reshape(seq_count * tok_rows, H * HD).astype(jnp.bfloat16)
    )
    y_attn = jnp.einsum("te,de->td", attn_b, full_out, preferred_element_type=jnp.float32)
    residual, back_attn = jax.vjp(add_branch, y_attn, flat, gain_attn)
    normed_two, back_two = jax.vjp(rms_scale, residual, gain_pre)
    normed_two_b = normed_two.astype(jnp.bfloat16)
    gate_up = jnp.dot(normed_two_b, full_gu, preferred_element_type=jnp.float32)
    hidden, back_act = jax.vjp(activate, gate_up)
    hidden_b = hidden.astype(jnp.bfloat16)
    branch = jnp.einsum("tf,df->td", hidden_b, full_down, preferred_element_type=jnp.float32)
    output, back_out = jax.vjp(add_branch, branch, residual, gain_post)
    result = output.astype(jnp.bfloat16).reshape(tokens.shape)
    seed_grad = cotangent.reshape(seq_count * tok_rows, D).astype(jnp.float32)
    d_branch, d_resid_a, d_gain_post = back_out(seed_grad)
    d_branch_b = d_branch.astype(jnp.bfloat16)
    grad_down = jnp.einsum("td,tf->df", d_branch_b, hidden_b, preferred_element_type=jnp.float32)
    d_hidden = jnp.einsum("td,df->tf", d_branch_b, full_down, preferred_element_type=jnp.float32)
    (d_gate_up,) = back_act(d_hidden)
    d_gate_up_b = d_gate_up.astype(jnp.bfloat16)
    grad_gu = jnp.einsum("td,tf->df", normed_two_b, d_gate_up_b, preferred_element_type=jnp.float32)
    d_normed_two = jnp.einsum("tf,df->td", d_gate_up_b, full_gu, preferred_element_type=jnp.float32)
    d_resid_b, d_gain_pre = back_two(d_normed_two)
    d_y_attn, d_flat_a, d_gain_attn = back_attn(d_resid_a + d_resid_b)
    d_y_attn_b = d_y_attn.astype(jnp.bfloat16)
    grad_out = jnp.einsum("td,te->de", d_y_attn_b, attn_b, preferred_element_type=jnp.float32)
    d_attn_rows = jnp.einsum(
        "td,de->te", d_y_attn_b, full_out, preferred_element_type=jnp.float32
    ).astype(jnp.bfloat16)
    d_attn = d_attn_rows.reshape(seq_count, tok_rows, H, HD).transpose(0, 2, 1, 3)
    row_dot = jnp.sum(d_attn.astype(jnp.float32) * attn_out, axis=-1)

    d_probs = jnp.einsum(
        "shrd,snd->shrn", d_attn, value_piece, preferred_element_type=jnp.float32
    )
    d_scores = (soft_b.astype(jnp.float32) * (d_probs - row_dot[..., None])).astype(jnp.bfloat16)
    d_key = (
        jnp.einsum("shrn,shrd->snd", d_scores, query_b, preferred_element_type=jnp.float32)
        * score_scale
    )
    d_value = jnp.einsum("shrn,shrd->snd", soft_b, d_attn, preferred_element_type=jnp.float32)
    d_key_value_all = jnp.concatenate([d_key, d_value], axis=-1).astype(jnp.bfloat16)
    if kernels:
        final_out, final_down, final_gu, d_key_value = scatter(
            (
                grad_out.astype(jnp.bfloat16),
                grad_down.astype(jnp.bfloat16),
                grad_gu.astype(jnp.bfloat16),
            ),
            (True, True, False),
            d_key_value_all,
            2,
            "scatter_rest",
        )
    else:
        final_out, final_down, final_gu = (
            scatter_all(grad_out),
            scatter_all(grad_down),
            scatter_all(grad_gu),
        )
        d_key_value = lax.psum_scatter(
            d_key_value_all, "ctx", scatter_dimension=1, tiled=True
        ).astype(jnp.float32)
    grad_key, grad_value = d_key_value[..., :HD], d_key_value[..., HD:]
    grad_query = (
        jnp.einsum("shrn,snd->shrd", d_scores, key_piece, preferred_element_type=jnp.float32)
        * score_scale
    )
    d_projected, d_gain_query, d_gain_key = back_prep((grad_query, grad_key, grad_value))
    d_projected_b = d_projected.astype(jnp.bfloat16)
    grad_qkv = jnp.einsum("td,te->de", normed_b, d_projected_b, preferred_element_type=jnp.float32)
    d_normed = jnp.einsum("te,de->td", d_projected_b, full_qkv, preferred_element_type=jnp.float32)
    d_flat_b, d_gain_in = back_one(d_normed)
    grad_tokens = (d_flat_a + d_flat_b).reshape(tokens.shape)
    grad_gain_all = jnp.concatenate(
        [d_gain_in, d_gain_attn, d_gain_pre, d_gain_post, d_gain_query, d_gain_key]
    )
    if kernels:
        gain_terms = grad_gain_all.reshape(group_count, ctx_size, 1, gain_count)
        gain_terms = jnp.pad(gain_terms, ((0, 0), (0, 0), (0, 7), (0, 128 - gain_count)))
        gain_terms = gain_terms.transpose(1, 2, 0, 3).reshape(ctx_size * 8, group_count * 128)
        gain_sum, final_qkv = scatter(
            (gain_terms, grad_qkv.astype(jnp.bfloat16)), (False, True), None, 3, "scatter_qkv"
        )
        final_gains = gain_sum[0, :gain_count]
    else:
        final_qkv = scatter_all(grad_qkv)
        final_gains = lax.psum_scatter(
            grad_gain_all, ("batch", "ctx"), scatter_dimension=0, tiled=True
        )
    return (
        result,
        grad_tokens,
        final_qkv,
        final_out.T,
        final_gu,
        final_down.T,
        final_gains,
    )


def solution(mesh):
    in_specs = (
        P("batch", "ctx", None),
        P("ctx", "batch"),
        P("batch", "ctx"),
        P("ctx", "batch"),
        P("batch", "ctx"),
        P(("batch", "ctx")),
        P(),
        P("batch", "ctx", None),
    )
    out_specs = (
        P("batch", "ctx", None),
        P("batch", "ctx", None),
        P("ctx", "batch"),
        P("batch", "ctx"),
        P("ctx", "batch"),
        P("batch", "ctx"),
        P(("batch", "ctx")),
    )
    return jax.shard_map(body, mesh=mesh, in_specs=in_specs, out_specs=out_specs, check_vma=False)
```
